512 devices in a mesh: lon: 32 (over z_lo, y, core), lat: 4 (over z_hi), exp: 4 (over x).
Axes of the slice: x: 4, y: 8, z: 8 (z_hi: 4, z_lo: 2; z = z_hi * 2 + z_lo), core: 2. Of those that a mesh axis runs over, the one named last changes fastest.
Arguments:
- tokens: bfloat16 [8, 24, 384, 1024], P('exp', 'lat', 'lon'), may hold values from -6 to 6
- queries: bfloat16 [8, 24, 384, 1024], P('exp', 'lat', 'lon'), may hold values from -7 to 7
- keys: bfloat16 [8, 24, 384, 1024], P('exp', 'lat', 'lon'), may hold values from -7 to 7
- values: bfloat16 [8, 24, 384, 1024], P('exp', 'lat', 'lon'), may hold values from -24 to 24
- shift_lat: int32 [1], replicated, may hold values from 1 to 5
- shift_lon: int32 [1], replicated, may hold values from 1 to 11
- norm_gain: float32 [1024], replicated, may hold values from 0.5 to 2
- w_router: bfloat16 [1024, 32], replicated, may hold values from -0.1875 to 0.1875
- routes: int32 [4, 4, 32, 144, 2], P('exp', 'lat', 'lon'), may hold values from 0 to 31, all different within a row; in each aligned block of 144 rows (0 to 143, 144 to 287, ..., all dimensions but the last counted through in order) at most 12 rows name the same one
- w_gate: bfloat16 [32, 1024, 2048], P('lon', None, 'exp'), may hold values from -0.1875 to 0.1875
- w_up: bfloat16 [32, 1024, 2048], P('lon', None, 'exp'), may hold values from -0.1875 to 0.1875
- w_down: bfloat16 [32, 1024, 2048], P('lon', None, 'exp'), may hold values from -0.125 to 0.125
Outputs:
- layer_out: bfloat16 [8, 24, 384, 1024], P('exp', 'lat', 'lon')
The draws below stay inside these ranges and needn't reach their ends.
Inputs may be any that keep to these rules, and one draw needn't show every extreme that they name: Each cell names two different experts. Among the 144 cells routes[i, j, m] no expert is named more than 12 times, and in some such block one is named exactly 12 times.
All inputs are finite; a program needn't handle non-finite values.
Results may differ from the reference program's by a relative error of at most 0.008.
Values may be sent and summed in bfloat16 or wider, within the bound.
A program may use at most 128 MiB of HBM per device.

```python
import math
import jax
import jax.numpy as jnp
import numpy as np
from jax import lax

HEADS = 32
HEAD_DIM = 32
D = 1024
FF = 2048
EXPERTS = 32
WIN_LEV = 2
WIN_LAT = 6
WIN_LON = 12
LON_DEV = 12
TOK_DEV = 144
CAP = 12
LEVELS = 8
NLAT = 24
NLON = 384
N_LON = 32
N_LAT = 4
N_EXP = 4


def draw_queries(key, part):
    key = jax.random.fold_in(key, 7)
    drawn = jnp.clip(jax.random.normal(key, (LEVELS, NLAT, NLON, D), jnp.float32), -6.0, 6.0)
    return drawn.reshape(LEVELS, NLAT, NLON, D).astype(jnp.bfloat16)


def draw_keys(key, part):
    key = jax.random.fold_in(key, 8)
    drawn = jnp.clip(jax.random.normal(key, (LEVELS, NLAT, NLON, D), jnp.float32), -6.0, 6.0)
    return drawn.reshape(LEVELS, NLAT, NLON, D).astype(jnp.bfloat16)


def levels(stream_key, extent, cuts, low, high):
    def one(axis_at, parts):
        steps = jax.random.uniform(jax.random.fold_in(jax.random.fold_in(stream_key, 6), axis_at), (parts,), jnp.float32, low / len(cuts), high / len(cuts))
        return jnp.repeat(jnp.exp(steps), extent[axis_at] // parts).reshape((-1,) + (1,) * (len(extent) - axis_at - 1))

    loudness = one(*cuts[0])
    for cut in cuts[1:]:
        loudness = loudness * one(*cut)
    return loudness


def routed_block(rng, own, number, rows, amount, top, reach, slope):
    ranking = jax.random.permutation(rng, amount)
    crowded, usual = shares(amount, rows * top, reach, slope, True), shares(amount, rows * top, reach, slope, False)
    places = jnp.arange(amount)

    def named(lengths, turn):
        used = int((lengths > 0).sum())
        fixed = max(1, used // 4)
        passed = fixed + (places - fixed + turn * (used - fixed)) % max(1, amount - fixed)
        return jnp.zeros((amount,), jnp.int32).at[ranking[jnp.where(places < fixed, places, passed)]].set(jnp.asarray(lengths, jnp.int32))

    lengths = jnp.where(number % 4 == 0, named(crowded, number // 4), named(usual, number - number // 4 - 1))
    mixed = jax.random.permutation(jax.random.fold_in(own, 3), amount)
    source_of, receiver = mixed[0:amount // 2 * 2:2], mixed[1:amount // 2 * 2:2]
    room = jnp.minimum(lengths[source_of] - 1, reach - lengths[receiver]) // 2
    room = jnp.where((source_of == ranking[0]) | (receiver == ranking[0]) | (lengths[receiver] == 0), 0, jnp.maximum(room, 0))
    passed = jax.random.randint(jax.random.fold_in(own, 4), (amount // 2,), 0, 1 << 20) % (room + 1)
    lengths = lengths.at[source_of].add(-passed).at[receiver].add(passed)
    items = jnp.searchsorted(jnp.cumsum(lengths), jnp.arange(rows * top), side="right").astype(jnp.int32)
    grid = items.reshape(top, rows).T
    grid = grid[jax.random.permutation(jax.random.fold_in(own, 1), rows)]
    turn = jax.random.randint(jax.random.fold_in(own, 2), (rows, 1), 0, top)
    return jnp.take_along_axis(grid, (jnp.arange(top)[None, :] + turn) % top, axis=1)


def shares(count, total, most, lean, full):
    loads = [(1 << 20) // math.isqrt(grade ** lean) + 1 for grade in range(1, count + 1)]
    largest = most if full else min(most, max(-(-total // count), total * loads[0] // sum(loads)))
    least = 1 if total - largest >= count - 1 else 0
    given, surplus = [largest] + [least] * (count - 1), total - largest - least * (count - 1)
    while surplus > 0:
        free = [i for i in range(1, count) if given[i] < largest] or [i for i in range(1, count) if given[i] < most]
        pool, left = sum([loads[i] for i in free]), surplus
        for i in free:
            addition = min(most - given[i], max(1, left * loads[i] // pool), surplus)
            given[i] = given[i] + addition
            surplus = surplus - addition
    return np.array(given)


def centred(own_key, dims, deviation, limit, cuts=(), kind=jnp.bfloat16):
    loudness = levels(own_key, dims, cuts, -0.22, 0.18) if cuts else 1.0
    values = jax.random.normal(own_key, dims, jnp.float32) * deviation * loudness
    return jnp.minimum(jnp.maximum(values, -limit), limit).astype(kind)


def setup_inputs(seed: int = 0) -> dict:
    seeds = jax.random.split(jax.random.key(seed), 13)
    tokens = centred(seeds[0], (LEVELS, NLAT, NLON, D), 1.0, 6.0, ((0, 4), (1, 4), (2, 32)))
    queries = draw_queries(jax.random.fold_in(seeds[12], 71), 0)
    keys = draw_keys(jax.random.fold_in(seeds[12], 71), 0)
    values = centred(seeds[3], (LEVELS, NLAT, NLON, D), 4.0, 24.0, ((0, 4), (1, 4), (2, 32)))
    shift_lat = jax.random.randint(seeds[4], (1,), 1, WIN_LAT).astype(jnp.int32)
    shift_lon = jax.random.randint(seeds[5], (1,), 1, WIN_LON).astype(jnp.int32)
    norm_gain = jnp.clip(jnp.exp(jax.random.uniform(seeds[6], (D,), jnp.float32, math.log(0.5), math.log(2.0))), 0.5, 2.0)
    w_router = centred(seeds[7], (D, EXPERTS), D ** -0.5, 0.1875)
    routes_keys = jax.random.split(jax.random.fold_in(seeds[8], 1), N_EXP * N_LAT * N_LON * TOK_DEV // TOK_DEV)
    routes_turns = jax.random.permutation(jax.random.fold_in(seeds[8], 3), N_EXP * N_LAT * N_LON * TOK_DEV // TOK_DEV)
    routes = jax.vmap(lambda own, number: routed_block(jax.random.fold_in(seeds[8], 2), own, number, TOK_DEV, EXPERTS, 2, CAP, 2))(routes_keys, routes_turns).reshape((N_EXP, N_LAT, N_LON, TOK_DEV, 2))
    w_gate = centred(seeds[9], (EXPERTS, D, FF), D ** -0.5, 0.1875, ((0, 32), (2, 4)))
    w_up = centred(seeds[10], (EXPERTS, D, FF), D ** -0.5, 0.1875, ((0, 32), (2, 4)))
    w_down = centred(seeds[11], (EXPERTS, D, FF), FF ** -0.5, 0.125, ((0, 32), (2, 4)))
    return dict(tokens=tokens, queries=queries, keys=keys, values=values, shift_lat=shift_lat, shift_lon=shift_lon, norm_gain=norm_gain, w_router=w_router, routes=routes, w_gate=w_gate, w_up=w_up, w_down=w_down)


def window_split(array_in, row_windows, col_windows):
    tail = array_in.shape[3:]
    level_windows = LEVELS // WIN_LEV
    shaped = array_in.reshape((level_windows, WIN_LEV, row_windows, WIN_LAT, col_windows, WIN_LON) + tail)
    order = (4, 0, 2, 1, 3, 5) + tuple(range(6, 6 + len(tail)))
    return shaped.transpose(order).reshape((col_windows, level_windows * row_windows, WIN_LEV * WIN_LAT * WIN_LON) + tail)

def window_merge(array_in, row_windows, col_windows):
    level_windows = LEVELS // WIN_LEV
    width = array_in.shape[-1]
    shaped = array_in.reshape(col_windows, level_windows, row_windows, WIN_LEV, WIN_LAT, WIN_LON, width)
    return shaped.transpose(1, 3, 2, 4, 0, 5, 6).reshape(LEVELS, row_windows * WIN_LAT, col_windows * WIN_LON, width)

def to_devices(array_in):
    width = array_in.shape[-1]
    shaped = array_in.reshape(N_EXP, WIN_LEV, N_LAT, WIN_LAT, N_LON, LON_DEV, width)
    return shaped.transpose(0, 2, 4, 1, 3, 5, 6).reshape(N_EXP * N_LAT * N_LON, TOK_DEV, width)

def from_devices(array_in):
    width = array_in.shape[-1]
    shaped = array_in.reshape(N_EXP, N_LAT, N_LON, WIN_LEV, WIN_LAT, LON_DEV, width)
    return shaped.transpose(0, 3, 1, 4, 2, 5, 6).reshape(LEVELS, NLAT, NLON, width)

def reference(tokens, queries, keys, values, shift_lat, shift_lon, norm_gain, w_router, routes, w_gate, w_up, w_down):
    lat_shift = shift_lat[0].astype(jnp.int32)
    lon_shift = shift_lon[0].astype(jnp.int32)
    row_windows = NLAT // WIN_LAT + 1
    col_windows = NLON // WIN_LON
    padded_rows = NLAT + WIN_LAT

    def prepare(array_in):
        rolled = jnp.roll(array_in, lon_shift, axis=2)
        padded = jnp.pad(rolled, ((0, 0), (WIN_LAT, WIN_LAT), (0, 0), (0, 0)))
        return lax.dynamic_slice_in_dim(padded, (WIN_LAT - lat_shift).astype(jnp.int32), padded_rows, 1)
    row_global = jnp.arange(padded_rows, dtype=jnp.int32) - lat_shift
    row_valid = (row_global >= 0) & (row_global < NLAT)
    valid_cells = jnp.broadcast_to(row_valid[None, :, None, None], (LEVELS, padded_rows, NLON, 1))
    key_valid = window_split(valid_cells, row_windows, col_windows)[..., 0]

    def heads_of(array_in):
        split = window_split(prepare(array_in), row_windows, col_windows)
        return split.reshape(split.shape[:3] + (HEADS, HEAD_DIM))
    query_win = heads_of(queries)
    key_win = heads_of(keys)
    value_win = heads_of(values)
    score_scale = HEAD_DIM ** (-0.5)

    def attend_block(block):
        query_blk, key_blk, value_blk, valid_blk = block
        scores = jnp.einsum('bqhd,bkhd->bhqk', query_blk.astype(jnp.float32), key_blk.astype(jnp.float32)) * score_scale
        scores = jnp.where(valid_blk[:, None, None, :], scores, -1e+30)
        shifted = scores - lax.optimization_barrier(jnp.max(scores, axis=-1, keepdims=True))
        weights = jnp.exp(shifted)
        probs = (weights / lax.optimization_barrier(jnp.sum(weights, axis=-1, keepdims=True))).astype(jnp.bfloat16)
        return jnp.einsum('bhqk,bkhd->bqhd', probs.astype(jnp.float32), value_blk.astype(jnp.float32))
    attended = lax.map(attend_block, (query_win, key_win, value_win, key_valid))
    attended = window_merge(attended.reshape(attended.shape[:3] + (D,)), row_windows, col_windows)
    attended = lax.dynamic_slice_in_dim(attended, lat_shift, NLAT, 1)
    attended = jnp.roll(attended, -lon_shift, axis=2)
    mid = tokens.astype(jnp.float32) + attended
    mean_square = lax.optimization_barrier(jnp.mean(mid * mid, axis=-1, keepdims=True))
    normed = (mid * lax.rsqrt(mean_square + 1e-06) * norm_gain).astype(jnp.bfloat16)
    device_count = N_EXP * N_LAT * N_LON
    cells_dev = to_devices(normed)
    mid_dev = to_devices(mid)
    logits = jnp.dot(cells_dev.reshape(-1, D), w_router, preferred_element_type=jnp.float32)
    logits = logits.reshape(device_count, TOK_DEV, EXPERTS)
    chosen = routes.reshape(device_count, TOK_DEV, 2).astype(jnp.int32)
    picked = jnp.take_along_axis(logits, chosen, axis=2)
    gate_prob = jax.nn.sigmoid(picked)
    combine = gate_prob / lax.optimization_barrier(jnp.sum(gate_prob, axis=2, keepdims=True))
    flat_routes = chosen.reshape(device_count, 2 * TOK_DEV)
    onehot = (flat_routes[:, :, None] == jnp.arange(EXPERTS, dtype=jnp.int32)[None, None, :]).astype(jnp.int32)
    slot_index = lax.optimization_barrier(jnp.sum((jnp.cumsum(onehot, axis=1) - onehot) * onehot, axis=2))
    row_target = (jnp.arange(device_count, dtype=jnp.int32)[:, None] * CAP + slot_index).astype(jnp.int32)
    sources = jnp.broadcast_to(cells_dev[:, :, None, :], (device_count, TOK_DEV, 2, D)).reshape(device_count, 2 * TOK_DEV, D)
    buffers = jnp.zeros((EXPERTS, device_count * CAP, D), jnp.bfloat16).at[flat_routes, row_target].set(sources)
    slice_width = FF // N_EXP

    def run_expert(block):
        rows_in, gate_w, up_w, down_w = block
        gate_act = jnp.dot(rows_in, gate_w, preferred_element_type=jnp.float32)
        up_act = jnp.dot(rows_in, up_w, preferred_element_type=jnp.float32)
        hidden = (jax.nn.silu(gate_act) * up_act).astype(jnp.bfloat16)
        hidden_parts = hidden.reshape(-1, N_EXP, slice_width).astype(jnp.float32)
        down_parts = down_w.reshape(D, N_EXP, slice_width).astype(jnp.float32)
        partial_value = jnp.einsum('rnf,dnf->nrd', hidden_parts, down_parts)
        rounded = lax.optimization_barrier(partial_value.astype(jnp.bfloat16)).astype(jnp.float32)
        return lax.optimization_barrier(jnp.sum(rounded, axis=0)).astype(jnp.bfloat16)
    expert_out = lax.map(run_expert, (buffers, w_gate, w_up, w_down))
    returned = expert_out[flat_routes, row_target].reshape(device_count, TOK_DEV, 2, D)
    moe = lax.optimization_barrier(jnp.sum(combine[..., None] * returned.astype(jnp.float32), axis=2))
    layer_dev = (mid_dev + moe).astype(jnp.bfloat16)
    return from_devices(layer_dev)
```

```python
import jax
import jax.numpy as jnp
from jax import lax
from jax.experimental import pallas as pl
from jax.experimental.pallas import tpu as pltpu
from jax.sharding import PartitionSpec as P

MESH = pl.DeviceIdType.MESH
F32 = jnp.float32
BF16 = jnp.bfloat16

CELLS = 144
PADDED = 192
D = 1024
FB = 256
NF = D // FB
HEAD_DIM = 32
HEADS_FB = FB // HEAD_DIM
N_LON, N_LAT, N_EXP = 32, 4, 4
EXPERTS = 32
CAP = 12
GROUPS = 8
GROUP_ROWS = 4 * CAP
ORDER = ((0, 0), (1, 0), (0, 1), (0, 3), (1, 1), (1, 3), (0, 2), (1, 2))


def iota(shape, dim):
    return lax.broadcasted_iota(jnp.int32, shape, dim)


def div12(n):
    return (n * 43691) >> 19


def div24(n):
    return (n * 43691) >> 20


def hot(mask, dtype=BF16):
    return jnp.where(mask, 1.0, 0.0).astype(dtype)


def dot(a, b):
    return jnp.dot(a, b, preferred_element_type=F32)


def dot_nt(a, b):
    return lax.dot_general(a, b, (((1,), (1,)), ((), ())), preferred_element_type=F32)


def layer_kernel(
    slat, slon, tok, qry, key, val, gain, wr, routes, wg_hbm, wu_hbm, wd_hbm, out,
    wg, wu, wd, pad, kv_own, kv_up, kv_dn, tt, kv_l, kv_r, qx, win, mid, nrm,
    m_row, m_col, q_row, q_col, bias, swap, pick0, pick1, disp, hot0, hot1,
    sbuf, rbuf, z, pr, rlb, rab, bbuf, ybuf, comb,
    w_sem, lat_s, lat_r, lon_s, lon_r, a2a_s, a2a_r, ag_s, ag_r, fw_s, fw_r,
    rl_s, rl_r, ra_s, ra_r, bk_s, bk_r,
):
    me = lax.axis_index("lon")
    lat = lax.axis_index("lat")
    ex = lax.axis_index("exp")
    right, left = lax.rem(ex + 1, N_EXP), lax.rem(ex + N_EXP - 1, N_EXP)

    weights = [
        pltpu.make_async_copy(h, v, w_sem.at[n])
        for n, (h, v) in enumerate(((wg_hbm, wg), (wu_hbm, wu), (wd_hbm, wd)))
    ]
    for copy in weights:
        copy.start()

    barrier = pltpu.get_barrier_semaphore()

    @pl.loop(1, N_LON)
    def _(o):
        pl.semaphore_signal(
            barrier, inc=1, device_id={"lon": lax.rem(me + o, N_LON)}, device_id_type=MESH
        )

    for axis, at, count in (("lat", lat, N_LAT), ("exp", ex, N_EXP)):
        for o in (1, count - 1):
            pl.semaphore_signal(
                barrier, inc=1, device_id={axis: lax.rem(at + o, count)}, device_id_type=MESH
            )

    def remote(src, dst, send, recv, **where):
        return pltpu.make_async_remote_copy(
            src_ref=src, dst_ref=dst, send_sem=send, recv_sem=recv,
            device_id=where, device_id_type=MESH,
        )

    def lat_copy(way, a, f):
        rows, dst, to = (
            (pl.ds(16, 128), kv_up, lax.rem(lat + 1, N_LAT)),
            (pl.ds(0, 128), kv_dn, lax.rem(lat + N_LAT - 1, N_LAT)),
        )[way]
        return remote(
            kv_own.at[a, f, rows], dst.at[a, f, rows],
            lat_s.at[way, a, f], lat_r.at[way, a, f], lat=to,
        )

    def lon_copy(way, a, f):
        dst, to = ((kv_l, lax.rem(me + 1, N_LON)), (kv_r, lax.rem(me + N_LON - 1, N_LON)))[way]
        return remote(
            tt.at[a, f], dst.at[a, f], lon_s.at[way, a, f], lon_r.at[way, a, f], lon=to
        )

    pad[...] = jnp.zeros_like(pad)

    def dense(ref, natural):
        for i in range(12):
            pad[16 * i : 16 * i + 12, :] = ref[i]
        n, at = iota((CELLS, PADDED), 0), iota((CELLS, PADDED), 1)
        if natural:
            run = div12(n)
            source = 16 * run + (n - 12 * run)
        else:
            row = div24(n)
            rest = n - 24 * row
            lev = div12(rest)
            source = (lev * 6 + row) * 16 + (rest - 12 * lev)
        return dot(hot(source == at), pad[...])

    for a, ref in enumerate((key, val)):
        cells = dense(ref, False).astype(BF16)
        for f in range(NF):
            kv_own[a, f] = cells[:, f * FB : (f + 1) * FB]

    pl.semaphore_wait(barrier, N_LON - 1 + 4)
    for f in range(NF):
        for a in range(2):
            for way in range(2):
                lat_copy(way, a, f).start()

    cells = dense(qry, True)
    head_of = iota((CELLS, FB), 1) >> 5
    for f in range(NF):
        for h in range(HEADS_FB):
            qx[f, h * CELLS : (h + 1) * CELLS] = jnp.where(
                head_of == h, cells[:, f * FB : (f + 1) * FB], 0.0
            ).astype(BF16)
    cells = dense(tok, True)
    for f in range(NF):
        mid[f] = cells[:, f * FB : (f + 1) * FB]

    s, t = slat[0], slon[0]
    n = iota((CELLS, FB), 0)
    m_row[...] = hot(div24(n) < 6 - s, F32)
    m_col[...] = hot(n - 12 * div12(n) < 12 - t, F32)
    run = div12(n)
    q_row[...] = hot(run - 6 * (div12(run * 2)) < 6 - s, F32)
    q_col[...] = hot(n - 12 * run < 12 - t, F32)
    krow = div24(iota((CELLS, CELLS), 1))
    low = jnp.where(krow < 6 - s + 100 * lat, 0.0, -1e30)
    high = jnp.where(krow >= 6 - s - 100 * (N_LAT - 1 - lat), 0.0, -1e30)
    bias[...] = jnp.where(q_row[:, :CELLS] > 0.5, low, high)

    tri = hot(iota((CELLS, CELLS), 0) > iota((CELLS, CELLS), 1))
    eye = iota((CELLS, CELLS), 0) == iota((CELLS, CELLS), 1)
    e = iota((CELLS, EXPERTS), 1)
    before = jnp.zeros((1, EXPERTS), F32)
    spread = jnp.zeros((EXPERTS * CAP, CELLS), F32)
    for k, (one, pick) in enumerate(((hot0, pick0), (hot1, pick1))):
        chosen = jnp.broadcast_to(routes[:, k : k + 1], (CELLS, EXPERTS))
        oh = hot(chosen == e, F32)
        one[...] = oh
        slot = jnp.sum((dot(tri, oh.astype(BF16)) + before) * oh, axis=1, keepdims=True)
        before = before + jnp.sum(oh, axis=0, keepdims=True)
        pos = slot + CAP * jnp.sum(oh * e.astype(F32), axis=1, keepdims=True)
        pick[...] = hot(
            jnp.broadcast_to(pos, (CELLS, EXPERTS * CAP))
            == iota((CELLS, EXPERTS * CAP), 1).astype(F32)
        )
        pos_row = jnp.sum(
            jnp.where(eye, jnp.broadcast_to(pos, (CELLS, CELLS)), 0.0), axis=0, keepdims=True
        )
        spread = spread + hot(
            jnp.broadcast_to(pos_row, (EXPERTS * CAP, CELLS))
            == iota((EXPERTS * CAP, CELLS), 0).astype(F32),
            F32,
        )
    disp[...] = spread.astype(BF16)
    n, at = iota((PADDED, PADDED), 0), iota((PADDED, PADDED), 1)
    outer = div24(n) >> 1
    rest = n - 48 * outer
    inner = div12(rest)
    swap[...] = hot(48 * inner + 12 * outer + (rest - 12 * inner) == at)

    def own_rows(f):
        for a in range(2):
            for way in range(2):
                lat_copy(way, a, f).wait_recv()
            own, up, dn = (r[a, f].astype(F32) for r in (kv_own, kv_up, kv_dn))
            inside = m_row[...] > 0.5
            tt[a, f, 0:CELLS] = jnp.where(inside, own, up).astype(BF16)
            tt[a, f, CELLS : 2 * CELLS] = jnp.where(inside, dn, own).astype(BF16)
            for way in range(2):
                lon_copy(way, a, f).start()

    def attend(f):
        for a in range(2):
            for way in range(2):
                lon_copy(way, a, f).wait_recv()
            inside = m_col[...] > 0.5
            for r in range(2):
                own, lo, hi = (
                    x[a, f, r * CELLS : (r + 1) * CELLS].astype(F32) for x in (tt, kv_l, kv_r)
                )
                win[a, 2 * r] = jnp.where(inside, own, lo).astype(BF16)
                win[a, 2 * r + 1] = jnp.where(inside, hi, own).astype(BF16)
        spread_q = qx[f]
        s_w = [dot_nt(spread_q, win[0, w]) for w in range(4)]
        first_row, first_col = q_row[:, :CELLS] > 0.5, q_col[:, :CELLS] > 0.5
        probs, scale = [], []
        for h in range(HEADS_FB):
            part = [x[h * CELLS : (h + 1) * CELLS] for x in s_w]
            score = jnp.where(
                first_row,
                jnp.where(first_col, part[0], part[1]),
                jnp.where(first_col, part[2], part[3]),
            )
            score = score * HEAD_DIM ** (-0.5) + bias[...]
            weight = jnp.exp(score - jnp.max(score, axis=1, keepdims=True))
            scale.append(1.0 / jnp.sum(weight, axis=1, keepdims=True))
            probs.append(weight.astype(BF16))
        probs = jnp.concatenate(probs, axis=0)
        o_w = [dot(probs, win[1, w]) for w in range(4)]
        first_row, first_col = q_row[...] > 0.5, q_col[...] > 0.5
        total = mid[f]
        for h in range(HEADS_FB):
            part = [x[h * CELLS : (h + 1) * CELLS] for x in o_w]
            got = jnp.where(
                first_row,
                jnp.where(first_col, part[0], part[1]),
                jnp.where(first_col, part[2], part[3]),
            )
            total = total + jnp.where(head_of == h, got * scale[h], 0.0)
        mid[f] = total

    own_rows(0)

    @pl.loop(0, NF)
    def _(f):
        @pl.when(f < NF - 1)
        def _():
            own_rows(f + 1)

        attend(f)

    square = sum(jnp.sum(mid[f] * mid[f], axis=1, keepdims=True) for f in range(NF))
    inv = lax.rsqrt(square * (1.0 / D) + 1e-06)
    for f in range(NF):
        cols = slice(f * FB, (f + 1) * FB)
        nrm[:, cols] = (mid[f] * inv * gain[:, cols]).astype(BF16)
    logits = dot(nrm[...], wr[...])
    gates = [
        jax.nn.sigmoid(jnp.sum(logits * one[...], axis=1, keepdims=True)) for one in (hot0, hot1)
    ]
    for k in range(2):
        comb[k] = jnp.broadcast_to(gates[k] / (gates[0] + gates[1]), (CELLS, 128))

    zl, yp, sm = me // 16, lax.rem(me // 4, 4), lax.rem(me, 4)

    def group(i):
        dz, dy = ORDER[i]
        return lax.rem(zl + dz, 2) * 4 + lax.rem(yp + dy, 4)

    def a2a(d):
        return remote(sbuf.at[d], rbuf.at[me], a2a_s.at[d], a2a_r.at[me], lon=d)

    def a2a_from(d):
        return remote(sbuf.at[d], rbuf.at[d], a2a_s.at[d], a2a_r.at[d], lon=d)

    def back(d):
        return remote(sbuf.at[d], bbuf.at[me], bk_s.at[d], bk_r.at[me], lon=d)

    def back_from(d):
        return remote(sbuf.at[d], bbuf.at[d], bk_s.at[d], bk_r.at[d], lon=d)

    def stacked(rows):
        blocks = jnp.concatenate([rows[:, f * FB : (f + 1) * FB] for f in range(NF)], axis=0)
        return dot(swap[...], blocks).astype(BF16).reshape(4, GROUP_ROWS, FB)

    def unstacked(blocks):
        rows = dot(swap[...], blocks.reshape(PADDED, FB)).astype(BF16)
        return [rows[f * GROUP_ROWS : (f + 1) * GROUP_ROWS] for f in range(NF)]

    for i in range(GROUPS):
        g = group(i)
        routed = dot(disp[pl.ds(pl.multiple_of(g * GROUP_ROWS, 16), GROUP_ROWS)], nrm[...])
        sbuf[pl.ds(g * 4, 4)] = stacked(routed.astype(BF16))
        for o in range(4):
            d = g * 4 + lax.rem(sm + o, 4)
            if i == 0 and o == 0:
                rbuf[d] = sbuf[d]
            else:
                a2a(d).start()

    def ag(way, i):
        return remote(
            z.at[0, i], z.at[1 + way, i], ag_s.at[way, i], ag_r.at[way, i],
            exp=(right, left)[way],
        )

    def fw(i):
        way = i % 2
        return remote(
            z.at[1 + way, i], z.at[3, i], fw_s.at[i], fw_r.at[i], exp=(right, left)[way]
        )

    def forward(i):
        ag(0, i).wait_recv()
        ag(1, i).wait_recv()
        fw(i).start()

    for i in range(GROUPS):
        g = group(i)
        for o in range(4):
            if not (i == 0 and o == 0):
                a2a_from(g * 4 + lax.rem(sm + o, 4)).wait_recv()
        for f, rows in enumerate(unstacked(rbuf[pl.ds(g * 4, 4)])):
            z[0, i, :, f * FB : (f + 1) * FB] = rows
        ag(0, i).start()
        ag(1, i).start()
        if i >= 2:
            forward(i - 2)

    for copy in weights:
        copy.wait()

    def ffn(plane, half):
        rows = z[plane, 4 * half : 4 * half + 4].reshape(PADDED, D)
        gate = dot(rows, wg[...])
        up = dot(rows, wu[...])
        hidden = (gate / (1.0 + jnp.exp(-gate)) * up).astype(BF16)
        down = dot_nt(hidden, wd[...]).astype(BF16)
        pr[plane, 4 * half : 4 * half + 4] = down.reshape(4, GROUP_ROWS, D)

    def rl(i):
        return remote(
            pr.at[3, i], rlb.at[i], rl_s.at[i], rl_r.at[i], exp=(right, left)[i % 2]
        )

    def ra(way, i):
        return remote(
            pr.at[2 - way, i], rab.at[way, i], ra_s.at[way, i], ra_r.at[way, i],
            exp=(right, left)[way],
        )

    def halves(half):
        return range(4 * half, 4 * half + 4)

    def direct(half):
        for i in halves(half):
            ra(1 - i % 2, i).start()

    def relay(half):
        for i in halves(half):
            fw(i).wait_recv()
        ffn(3, half)
        for i in halves(half):
            rl(i).start()

    def relayed(half):
        for i in halves(half):
            way = i % 2
            rl(i).wait_recv()
            pr[2 - way, i] = (pr[2 - way, i].astype(F32) + rlb[i].astype(F32)).astype(BF16)
            ra(way, i).start()

    def finish(half):
        for i in halves(half):
            ra(0, i).wait_recv()
            ra(1, i).wait_recv()
            rows = pr[0, i].astype(F32) + rab[0, i].astype(F32) + rab[1, i].astype(F32)
            blocks = stacked(rows.astype(BF16))
            g = group(i)
            if i == 0:
                for o in range(1, 4):
                    a2a(g * 4 + lax.rem(sm + o, 4)).wait_send()
            else:
                for o in range(4):
                    a2a(g * 4 + lax.rem(sm + o, 4)).wait_send()
            sbuf[pl.ds(g * 4, 4)] = blocks
            for o in range(4):
                d = g * 4 + lax.rem(sm + o, 4)
                if i == 0 and o == 0:
                    bbuf[d] = sbuf[d]
                else:
                    back(d).start()

    ffn(0, 0)
    forward(6)
    ffn(1, 0)
    ffn(2, 0)
    direct(0)
    forward(7)
    relay(0)
    ffn(0, 1)
    ffn(1, 1)
    ffn(2, 1)
    relayed(0)
    direct(1)
    relay(1)
    finish(0)
    relayed(1)
    finish(1)

    for i in range(GROUPS):
        g = group(i)
        for o in range(4):
            if not (i == 0 and o == 0):
                back_from(g * 4 + lax.rem(sm + o, 4)).wait_recv()
        at = pl.ds(pl.multiple_of(g * GROUP_ROWS, 16), GROUP_ROWS)
        for f, rows in enumerate(unstacked(bbuf[pl.ds(g * 4, 4)])):
            ybuf[at, f * FB : (f + 1) * FB] = rows
    n, at = iota((PADDED, CELLS), 0), iota((PADDED, CELLS), 1)
    run, col = n >> 4, n & 15
    widen = hot((run * 12 + col == at) & (col < 12))
    for f in range(NF):
        cols = slice(f * FB, (f + 1) * FB)
        moe = comb[0, :, :1] * dot(pick0[...], ybuf[:, cols])
        moe = moe + comb[1, :, :1] * dot(pick1[...], ybuf[:, cols])
        full = dot(widen, (mid[f] + moe).astype(BF16)).astype(BF16)
        for i in range(12):
            out[i, :, cols] = full[16 * i : 16 * i + 12]

    @pl.loop(0, NF)
    def _(f):
        for a in range(2):
            for way in range(2):
                lat_copy(way, a, f).wait_send()
                lon_copy(way, a, f).wait_send()

    for i in range(GROUPS):
        fw(i).wait_send()
        rl(i).wait_send()
        for way in range(2):
            ag(way, i).wait_send()
            ra(way, i).wait_send()

    @pl.loop(1, N_LON)
    def _(o):
        back(lax.rem(me + o, N_LON)).wait_send()


def shards(
    tokens, queries, keys, values, shift_lat, shift_lon, norm_gain, w_router, routes,
    w_gate, w_up, w_down,
):
    def flat(x):
        return x.reshape(12, 12, D)

    smem = pl.BlockSpec(memory_space=pltpu.SMEM)
    vmem = pl.BlockSpec(memory_space=pltpu.VMEM)
    hbm = pl.BlockSpec(memory_space=pl.ANY)
    dma = pltpu.SemaphoreType.DMA
    kv = pltpu.VMEM((2, NF, CELLS, FB), BF16)
    kv2 = pltpu.VMEM((2, NF, 2 * CELLS, FB), BF16)
    blocks = pltpu.VMEM((N_LON, GROUP_ROWS, FB), BF16)
    planes = pltpu.VMEM((N_EXP, GROUPS, GROUP_ROWS, D), BF16)
    mask = pltpu.VMEM((CELLS, FB), F32)
    ff = w_gate.shape[2]
    out = pl.pallas_call(
        layer_kernel,
        out_shape=jax.ShapeDtypeStruct((12, 12, D), BF16),
        in_specs=[smem] * 2 + [vmem] * 7 + [hbm] * 3,
        out_specs=vmem,
        scratch_shapes=[
            pltpu.VMEM((D, ff), BF16), pltpu.VMEM((D, ff), BF16), pltpu.VMEM((D, ff), BF16),
            pltpu.VMEM((PADDED, D), BF16),
            kv, kv, kv, kv2, kv2, kv2,
            pltpu.VMEM((NF, HEADS_FB * CELLS, FB), BF16),
            pltpu.VMEM((2, 4, CELLS, FB), BF16),
            pltpu.VMEM((NF, CELLS, FB), F32),
            pltpu.VMEM((CELLS, D), BF16),
            mask, mask, mask, mask,
            pltpu.VMEM((CELLS, CELLS), F32),
            pltpu.VMEM((PADDED, PADDED), BF16),
            pltpu.VMEM((CELLS, EXPERTS * CAP), BF16), pltpu.VMEM((CELLS, EXPERTS * CAP), BF16),
            pltpu.VMEM((EXPERTS * CAP, CELLS), BF16),
            pltpu.VMEM((CELLS, EXPERTS), F32), pltpu.VMEM((CELLS, EXPERTS), F32),
            blocks, blocks,
            planes, planes,
            pltpu.VMEM((GROUPS, GROUP_ROWS, D), BF16),
            pltpu.VMEM((2, GROUPS, GROUP_ROWS, D), BF16),
            blocks,
            pltpu.VMEM((EXPERTS * CAP, D), BF16),
            pltpu.VMEM((2, CELLS, 128), F32),
            dma((3,)),
            dma((2, 2, NF)), dma((2, 2, NF)), dma((2, 2, NF)), dma((2, 2, NF)),
            dma((N_LON,)), dma((N_LON,)),
            dma((2, GROUPS)), dma((2, GROUPS)), dma((GROUPS,)), dma((GROUPS,)),
            dma((GROUPS,)), dma((GROUPS,)), dma((2, GROUPS)), dma((2, GROUPS)),
            dma((N_LON,)), dma((N_LON,)),
        ],
        compiler_params=pltpu.CompilerParams(
            collective_id=0, has_side_effects=True, vmem_limit_bytes=56 * 1024 * 1024
        ),
        cost_estimate=pl.CostEstimate(
            flops=6_000_000_000, bytes_accessed=8_000_000, transcendentals=2_000_000
        ),
    )(
        shift_lat, shift_lon, flat(tokens), flat(queries), flat(keys), flat(values),
        norm_gain.reshape(1, D), w_router, routes.reshape(CELLS, 2),
        w_gate.reshape(D, ff), w_up.reshape(D, ff), w_down.reshape(D, ff),
    )
    return out.reshape(tokens.shape)


def solution(mesh):
    cells = P("exp", "lat", "lon", None)
    weights = P("lon", None, "exp")
    in_specs = (
        cells, cells, cells, cells, P(), P(), P(), P(),
        P("exp", "lat", "lon", None, None), weights, weights, weights,
    )
    return jax.shard_map(
        shards, mesh=mesh, in_specs=in_specs, out_specs=cells, check_vma=False
    )
```

```python
import functools

import jax
import jax.numpy as jnp
from jax import lax
from jax.experimental import pallas as pl
from jax.experimental.pallas import tpu as pltpu
from jax.sharding import PartitionSpec as P

MESH = pl.DeviceIdType.MESH
F32 = jnp.float32
BF16 = jnp.bfloat16

CELLS = 144
D = 1024
LANES = 128
RUNS = CELLS * D // LANES
FB = 256
NF = D // FB
HEAD_DIM = 32
HEADS_FB = FB // HEAD_DIM
N_LON, N_LAT, N_EXP = 32, 4, 4
EXPERTS = 32
CAP = 12
GROUPS = 8
GROUP_ROWS = 4 * CAP
STACK = 4 * GROUP_ROWS
HALF = 72
SENT = 224
BACK = 80
ORDER = ((0, 0), (1, 0), (0, 1), (0, 3), (1, 1), (1, 3), (0, 2), (1, 2))


def iota(shape, dim):
    return lax.broadcasted_iota(jnp.int32, shape, dim)


def div12(n):
    return (n * 43691) >> 19


def div24(n):
    return (n * 43691) >> 20


def hot(mask, dtype=BF16):
    return jnp.where(mask, 1.0, 0.0).astype(dtype)


def dot(a, b):
    return jnp.dot(a, b, preferred_element_type=F32)


def dot_nt(a, b):
    return lax.dot_general(a, b, (((1,), (1,)), ((), ())), preferred_element_type=F32)


def layer_kernel(
    side, slat, slon, tok, qry, key, val, gain, wr, routes, wg_hbm, wu_hbm, wd_hbm, out,
    wg, wu, wd, qkv, sent, got, kv, kv_up, kv_dn, qx, ret, ret_got, mid, nrm,
    m_low, m_high, m_row, m_in, bias, pick_lon, put_lon, pick_ret, put_ret, untile, swap,
    pick0, pick1, disp, hot0, hot1, sbuf, rbuf, z, pr, rlb, rab, bbuf, ybuf, comb,
    w_sem, lat_s, lat_r, lon_s, lon_r, ret_s, ret_r, a2a_s, a2a_r, ag_s, ag_r, fw_s, fw_r,
    rl_s, rl_r, ra_s, ra_r, bk_s, bk_r,
):
    me = lax.axis_index("lon")
    lat = lax.axis_index("lat")
    ex = lax.axis_index("exp")
    right, left = lax.rem(ex + 1, N_EXP), lax.rem(ex + N_EXP - 1, N_EXP)
    east, west = lax.rem(me + 1, N_LON), lax.rem(me + N_LON - 1, N_LON)
    first = 0 if side else 12

    barrier = pltpu.get_barrier_semaphore()

    @pl.loop(1, N_LON)
    def _(o):
        pl.semaphore_signal(
            barrier, inc=1, device_id={"lon": lax.rem(me + o, N_LON)}, device_id_type=MESH
        )

    for axis, at, count in (("lat", lat, N_LAT), ("exp", ex, N_EXP)):
        for o in (1, count - 1):
            pl.semaphore_signal(
                barrier, inc=1, device_id={axis: lax.rem(at + o, count)}, device_id_type=MESH
            )

    weights = [
        pltpu.make_async_copy(h, v, w_sem.at[n])
        for n, (h, v) in enumerate(((wg_hbm, wg), (wu_hbm, wu), (wd_hbm, wd)))
    ]
    for copy in weights:
        copy.start()

    def remote(src, dst, send, recv, **where):
        return pltpu.make_async_remote_copy(
            src_ref=src, dst_ref=dst, send_sem=send, recv_sem=recv,
            device_id=where, device_id_type=MESH,
        )

    def lon_copy(f):
        return remote(sent.at[f], got.at[f], lon_s.at[f], lon_r.at[f], lon=(east, west)[side])

    def ret_copy(f):
        return remote(ret.at[f], ret_got.at[f], ret_s.at[f], ret_r.at[f], lon=(west, east)[side])

    def lat_copy(way, f):
        rows, dst, to = (
            (pl.ds(16, 128), kv_up, lax.rem(lat + 1, N_LAT)),
            (pl.ds(0, 128), kv_dn, lax.rem(lat + N_LAT - 1, N_LAT)),
        )[way]
        return remote(
            kv.at[f, :, rows], dst.at[f, :, rows], lat_s.at[way, f], lat_r.at[way, f], lat=to
        )

    n, at = iota((LANES, LANES), 0), iota((LANES, LANES), 1)
    untile[...] = hot(((n & 15) >> 1) * 16 + (n >> 4) * 2 + (n & 1) == at)

    def dense(ref, store):
        for b in range(CELLS // 16):
            rows = dot(untile[...], ref[b * LANES : (b + 1) * LANES])
            for j in range(D // LANES):
                f, c = j // 2, (j % 2) * LANES
                store(f, slice(b * 16, b * 16 + 16), slice(c, c + LANES), rows[j * 16 : j * 16 + 16])

    s, t = slat[0], slon[0]
    for a, ref in enumerate((qry, key, val)):

        def to_qkv(f, rows, cols, part, a=a):
            qkv[f, a * CELLS + rows.start : a * CELLS + rows.stop, cols] = part.astype(BF16)

        dense(ref, to_qkv)
    n, at = iota((SENT, 3 * CELLS), 0), iota((SENT, 3 * CELLS), 1)
    a = jnp.where(n >= HALF, 1, 0) + jnp.where(n >= 2 * HALF, 1, 0)
    m = n - HALF * a
    row = div12(m)
    source = a * CELLS + row * 24 + first + (m - 12 * row)
    pick_lon[...] = hot((source == at) & (n < 3 * HALF))
    for f in range(NF):
        sent[f] = dot(pick_lon[...], qkv[f]).astype(BF16)

    pl.semaphore_wait(barrier, N_LON - 1 + 4)
    for f in range(NF):
        lon_copy(f).start()

    n = iota((CELLS, FB), 0)
    row = div24(n)
    rest = n - 24 * row
    at_top, at_bottom = jnp.where(lat == 0, 100, 0), jnp.where(lat == N_LAT - 1, 100, 0)
    m_row[...] = hot(row < 6 - s, F32)
    m_low[...] = hot(row < 6 - s + at_top, F32)
    m_high[...] = hot(row < 6 - s - at_bottom, F32)
    columns = (rest >> 1) < 12 - t
    m_in[...] = hot(columns, F32) if side == 0 else 1.0 - hot(columns, F32)

    shape = (3 * CELLS, 3 * CELLS + SENT)
    n, at = iota(shape, 0), iota(shape, 1)
    a = jnp.where(n >= CELLS, 1, 0) + jnp.where(n >= 2 * CELLS, 1, 0)
    m = n - CELLS * a
    row = div24(m)
    rest = m - 24 * row
    inside = (rest >> 1) < 12 - t if side == 0 else (rest >> 1) >= 12 - t
    put_lon[...] = hot(
        at == jnp.where(inside, n, 3 * CELLS + HALF * a + row * 12 + rest - first)
    )
    head_of = iota((CELLS, FB), 1) >> 5

    def own_columns(f):
        lon_copy(f).wait_recv()
        cells = dot(put_lon[...], jnp.concatenate([qkv[f], got[f]], axis=0))
        kv[f, 0] = cells[CELLS : 2 * CELLS].astype(BF16)
        kv[f, 1] = cells[2 * CELLS :].astype(BF16)

        @pl.when(lat < N_LAT - 1)
        def _():
            lat_copy(0, f).start()

        @pl.when(lat > 0)
        def _():
            lat_copy(1, f).start()

        for h in range(HEADS_FB):
            qx[f, h * CELLS : (h + 1) * CELLS] = jnp.where(
                head_of == h, cells[:CELLS], 0.0
            ).astype(BF16)

    @pl.loop(0, NF)
    def _(f):
        own_columns(f)

    def to_mid(f, rows, cols, part):
        mid[f, rows, cols] = part

    dense(tok, to_mid)

    krow = div24(iota((CELLS, CELLS), 1))
    low = jnp.where(krow < 6 - s + 100 * lat, 0.0, -1e30)
    high = jnp.where(krow >= 6 - s - 100 * (N_LAT - 1 - lat), 0.0, -1e30)
    bias[...] = jnp.where(m_row[:, :CELLS] > 0.5, low, high)

    n, at = iota((BACK, CELLS), 0), iota((BACK, CELLS), 1)
    row = div12(n)
    pick_ret[...] = hot(row * 24 + first + (n - 12 * row) == at)
    n, at = iota((CELLS, BACK), 0), iota((CELLS, BACK), 1)
    row = div24(n)
    rest = n - 24 * row - first
    put_ret[...] = hot((row * 12 + rest == at) & (rest >= 0) & (rest < 12))

    tri = hot(iota((CELLS, CELLS), 0) > iota((CELLS, CELLS), 1))
    n, at = iota((CELLS, CELLS), 0), iota((CELLS, CELLS), 1)
    eye = n == at
    ordered = (n & 1) * HALF + (n >> 1) == at
    e = iota((CELLS, EXPERTS), 1).astype(F32)
    before = jnp.zeros((1, EXPERTS), F32)
    spread = jnp.zeros((EXPERTS * CAP, CELLS), F32)
    for k, (one, pick) in enumerate(((hot0, pick0), (hot1, pick1))):
        named = jnp.broadcast_to(routes[k : k + 1, :].astype(F32), (CELLS, CELLS))
        chosen = jnp.sum(jnp.where(ordered, named, 0.0), axis=1, keepdims=True)
        oh = hot(jnp.broadcast_to(chosen, (CELLS, EXPERTS)) == e, F32)
        one[...] = oh
        slot = jnp.sum((dot(tri, oh.astype(BF16)) + before) * oh, axis=1, keepdims=True)
        before = before + jnp.sum(oh, axis=0, keepdims=True)
        pos = slot + CAP * chosen
        pick[...] = hot(
            jnp.broadcast_to(pos, (CELLS, EXPERTS * CAP))
            == iota((CELLS, EXPERTS * CAP), 1).astype(F32)
        )
        pos_row = jnp.sum(
            jnp.where(eye, jnp.broadcast_to(pos, (CELLS, CELLS)), 0.0), axis=0, keepdims=True
        )
        spread = spread + hot(
            jnp.broadcast_to(pos_row, (EXPERTS * CAP, CELLS))
            == iota((EXPERTS * CAP, CELLS), 0).astype(F32),
            F32,
        )
    disp[...] = spread.astype(BF16)
    n, at = iota((STACK, STACK), 0), iota((STACK, STACK), 1)
    outer = div24(n) >> 1
    rest = n - 48 * outer
    inner = div12(rest)
    swap[...] = hot(48 * inner + 12 * outer + (rest - 12 * inner) == at)

    def attend(f):
        @pl.when(lat > 0)
        def _():
            lat_copy(0, f).wait_recv()

        @pl.when(lat < N_LAT - 1)
        def _():
            lat_copy(1, f).wait_recv()

        win = []
        for a in range(2):
            own, up, dn = (r[f, a].astype(F32) for r in (kv, kv_up, kv_dn))
            win.append(
                (
                    jnp.where(m_low[...] > 0.5, own, up).astype(BF16),
                    jnp.where(m_high[...] > 0.5, dn, own).astype(BF16),
                )
            )
        spread_q = qx[f]
        s_w = [dot_nt(spread_q, w) for w in win[0]]
        first_row = m_row[:, :CELLS] > 0.5
        probs, scale = [], []
        for h in range(HEADS_FB):
            part = [x[h * CELLS : (h + 1) * CELLS] for x in s_w]
            score = jnp.where(first_row, part[0], part[1]) * HEAD_DIM ** (-0.5) + bias[...]
            weight = jnp.exp(score - jnp.max(score, axis=1, keepdims=True))
            scale.append(1.0 / jnp.sum(weight, axis=1, keepdims=True))
            probs.append(weight.astype(BF16))
        probs = jnp.concatenate(probs, axis=0)
        o_w = [dot(probs, w) for w in win[1]]
        first_row = m_row[...] > 0.5
        total = jnp.zeros((CELLS, FB), F32)
        for h in range(HEADS_FB):
            part = [x[h * CELLS : (h + 1) * CELLS] for x in o_w]
            heads = jnp.where(first_row, part[0], part[1]) * scale[h]
            total = jnp.where(head_of == h, heads, total)
        ret[f] = dot(pick_ret[...], total.astype(BF16)).astype(BF16)
        ret_copy(f).start()
        mid[f] = mid[f] + jnp.where(m_in[...] > 0.5, total, 0.0)

    @pl.loop(0, NF)
    def _(f):
        attend(f)

    for f in range(NF):
        ret_copy(f).wait_recv()
        back_home = dot(put_ret[...], ret_got[f])
        mid[f] = mid[f] + jnp.where(m_in[...] > 0.5, 0.0, back_home)

    square = sum(jnp.sum(mid[f] * mid[f], axis=1, keepdims=True) for f in range(NF))
    inv = lax.rsqrt(square * (1.0 / D) + 1e-06)
    for f in range(NF):
        cols = slice(f * FB, (f + 1) * FB)
        nrm[:, cols] = (mid[f] * inv * gain[:, cols]).astype(BF16)
    logits = dot_nt(nrm[...], wr[...])
    gates = [
        jax.nn.sigmoid(jnp.sum(logits * one[...], axis=1, keepdims=True)) for one in (hot0, hot1)
    ]
    for k in range(2):
        comb[k] = jnp.broadcast_to(gates[k] / (gates[0] + gates[1]), (CELLS, 128))

    zl, yp, sm = me // 16, lax.rem(me // 4, 4), lax.rem(me, 4)

    def group(i):
        dz, dy = ORDER[i]
        return lax.rem(zl + dz, 2) * 4 + lax.rem(yp + dy, 4)

    def a2a(d):
        return remote(sbuf.at[d], rbuf.at[me], a2a_s.at[d], a2a_r.at[me], lon=d)

    def a2a_from(d):
        return remote(sbuf.at[d], rbuf.at[d], a2a_s.at[d], a2a_r.at[d], lon=d)

    def back(d):
        return remote(sbuf.at[d], bbuf.at[me], bk_s.at[d], bk_r.at[me], lon=d)

    def back_from(d):
        return remote(sbuf.at[d], bbuf.at[d], bk_s.at[d], bk_r.at[d], lon=d)

    def stacked(rows):
        blocks = jnp.concatenate([rows[:, f * FB : (f + 1) * FB] for f in range(NF)], axis=0)
        return dot(swap[...], blocks).astype(BF16).reshape(4, GROUP_ROWS, FB)

    def unstacked(blocks):
        rows = dot(swap[...], blocks.reshape(STACK, FB)).astype(BF16)
        return [rows[f * GROUP_ROWS : (f + 1) * GROUP_ROWS] for f in range(NF)]

    ybuf[...] = dot(disp[...], nrm[...]).astype(BF16)
    for i in range(GROUPS):
        g = group(i)
        sbuf[pl.ds(g * 4, 4)] = stacked(
            ybuf[pl.ds(pl.multiple_of(g * GROUP_ROWS, 16), GROUP_ROWS)]
        )
    rbuf[me] = sbuf[me]
    for i in range(GROUPS):
        g = group(i)
        for o in range(4):
            if not (i == 0 and o == 0):
                a2a(g * 4 + lax.rem(sm + o, 4)).start()

    def ag(way, i):
        return remote(
            z.at[0, i], z.at[1 + way, i], ag_s.at[way, i], ag_r.at[way, i],
            exp=(right, left)[way],
        )

    def fw(i):
        way = i % 2
        return remote(
            z.at[1 + way, i], z.at[3, i], fw_s.at[i], fw_r.at[i], exp=(right, left)[way]
        )

    def forward(i):
        ag(0, i).wait_recv()
        ag(1, i).wait_recv()
        fw(i).start()

    def ffn(plane, half):
        rows = z[plane, 4 * half : 4 * half + 4].reshape(STACK, D)
        gate = dot(rows, wg[...])
        up = dot(rows, wu[...])
        hidden = (gate / (1.0 + jnp.exp(-gate)) * up).astype(BF16)
        down = dot_nt(hidden, wd[...]).astype(BF16)
        pr[plane, 4 * half : 4 * half + 4] = down.reshape(4, GROUP_ROWS, D)

    def rl(i):
        return remote(
            pr.at[3, i], rlb.at[i], rl_s.at[i], rl_r.at[i], exp=(right, left)[i % 2]
        )

    def ra(way, i):
        return remote(
            pr.at[2 - way, i], rab.at[way, i], ra_s.at[way, i], ra_r.at[way, i],
            exp=(right, left)[way],
        )

    def halves(half):
        return range(4 * half, 4 * half + 4)

    def direct(half):
        for i in halves(half):
            ra(1 - i % 2, i).start()

    def relay(half):
        for i in halves(half):
            fw(i).wait_recv()
        ffn(3, half)
        for i in halves(half):
            rl(i).start()

    def relayed(half):
        for i in halves(half):
            way = i % 2
            rl(i).wait_recv()
            pr[2 - way, i] = (pr[2 - way, i].astype(F32) + rlb[i].astype(F32)).astype(BF16)
            ra(way, i).start()

    def finish(half):
        for i in halves(half):
            ra(0, i).wait_recv()
            ra(1, i).wait_recv()
            rows = pr[0, i].astype(F32) + rab[0, i].astype(F32) + rab[1, i].astype(F32)
            blocks = stacked(rows.astype(BF16))
            g = group(i)
            if i == 0:
                for o in range(1, 4):
                    a2a(g * 4 + lax.rem(sm + o, 4)).wait_send()
            else:
                for o in range(4):
                    a2a(g * 4 + lax.rem(sm + o, 4)).wait_send()
            sbuf[pl.ds(g * 4, 4)] = blocks
            for o in range(4):
                d = g * 4 + lax.rem(sm + o, 4)
                if i == 0 and o == 0:
                    bbuf[d] = sbuf[d]
                else:
                    back(d).start()

    for copy in weights:
        copy.wait()

    for i in range(GROUPS):
        g = group(i)
        for o in range(4):
            if not (i == 0 and o == 0):
                a2a_from(g * 4 + lax.rem(sm + o, 4)).wait_recv()
        for f, rows in enumerate(unstacked(rbuf[pl.ds(g * 4, 4)])):
            z[0, i, :, f * FB : (f + 1) * FB] = rows
        ag(0, i).start()
        ag(1, i).start()
        if i >= 2:
            forward(i - 2)
        if i >= 5:
            ffn(i - 5, 0)
    direct(0)
    forward(6)
    relay(0)
    forward(7)
    relay(1)
    ffn(1, 1)
    ffn(2, 1)
    direct(1)
    relayed(0)
    ffn(0, 1)
    finish(0)
    relayed(1)
    finish(1)

    for i in range(GROUPS):
        g = group(i)
        for o in range(4):
            if not (i == 0 and o == 0):
                back_from(g * 4 + lax.rem(sm + o, 4)).wait_recv()
        at = pl.ds(pl.multiple_of(g * GROUP_ROWS, 16), GROUP_ROWS)
        for f, rows in enumerate(unstacked(bbuf[pl.ds(g * 4, 4)])):
            ybuf[at, f * FB : (f + 1) * FB] = rows
    for f in range(NF):
        cols = slice(f * FB, (f + 1) * FB)
        moe = comb[0, :, :1] * dot(pick0[...], ybuf[:, cols])
        moe = moe + comb[1, :, :1] * dot(pick1[...], ybuf[:, cols])
        out[:, cols] = (mid[f] + moe).astype(BF16)
    for f in range(NF):
        lon_copy(f).wait_send()
        ret_copy(f).wait_send()

    @pl.when(lat < N_LAT - 1)
    def _():
        for f in range(NF):
            lat_copy(0, f).wait_send()

    @pl.when(lat > 0)
    def _():
        for f in range(NF):
            lat_copy(1, f).wait_send()

    for i in range(GROUPS):
        fw(i).wait_send()
        rl(i).wait_send()
        for way in range(2):
            ag(way, i).wait_send()
            ra(way, i).wait_send()

    @pl.loop(1, N_LON)
    def _(o):
        back(lax.rem(me + o, N_LON)).wait_send()


def shards(
    tokens, queries, keys, values, shift_lat, shift_lon, norm_gain, w_router, routes,
    w_gate, w_up, w_down,
):
    def flat(x):
        return x.reshape(2, 6, 12, D // LANES, LANES).transpose(1, 2, 3, 0, 4).reshape(RUNS, LANES)

    smem = pl.BlockSpec(memory_space=pltpu.SMEM)
    vmem = pl.BlockSpec(memory_space=pltpu.VMEM)
    hbm = pl.BlockSpec(memory_space=pl.ANY)
    dma = pltpu.SemaphoreType.DMA
    kv = pltpu.VMEM((NF, 2, CELLS, FB), BF16)
    lon = pltpu.VMEM((NF, SENT, FB), BF16)
    ret = pltpu.VMEM((NF, BACK, FB), BF16)
    blocks = pltpu.VMEM((N_LON, GROUP_ROWS, FB), BF16)
    planes = pltpu.VMEM((N_EXP, GROUPS, GROUP_ROWS, D), BF16)
    mask = pltpu.VMEM((CELLS, FB), F32)
    slots = EXPERTS * CAP
    ff = w_gate.shape[2]
    scratch = [
        pltpu.VMEM((D, ff), BF16), pltpu.VMEM((D, ff), BF16), pltpu.VMEM((D, ff), BF16),
        pltpu.VMEM((NF, 3 * CELLS, FB), BF16),
        lon, lon, kv, kv, kv,
        pltpu.VMEM((NF, HEADS_FB * CELLS, FB), BF16),
        ret, ret,
        pltpu.VMEM((NF, CELLS, FB), F32),
        pltpu.VMEM((CELLS, D), BF16),
        mask, mask, mask, mask,
        pltpu.VMEM((CELLS, CELLS), F32),
        pltpu.VMEM((SENT, 3 * CELLS), BF16), pltpu.VMEM((3 * CELLS, 3 * CELLS + SENT), BF16),
        pltpu.VMEM((BACK, CELLS), BF16), pltpu.VMEM((CELLS, BACK), BF16),
        pltpu.VMEM((LANES, LANES), BF16),
        pltpu.VMEM((STACK, STACK), BF16),
        pltpu.VMEM((CELLS, slots), BF16), pltpu.VMEM((CELLS, slots), BF16),
        pltpu.VMEM((slots, CELLS), BF16),
        pltpu.VMEM((CELLS, EXPERTS), F32), pltpu.VMEM((CELLS, EXPERTS), F32),
        blocks, blocks, planes, planes,
        pltpu.VMEM((GROUPS, GROUP_ROWS, D), BF16),
        pltpu.VMEM((2, GROUPS, GROUP_ROWS, D), BF16),
        blocks,
        pltpu.VMEM((slots, D), BF16),
        pltpu.VMEM((2, CELLS, 128), F32),
        dma((3,)),
        dma((2, NF)), dma((2, NF)), dma((NF,)), dma((NF,)), dma((NF,)), dma((NF,)),
        dma((N_LON,)), dma((N_LON,)),
        dma((2, GROUPS)), dma((2, GROUPS)), dma((GROUPS,)), dma((GROUPS,)),
        dma((GROUPS,)), dma((GROUPS,)), dma((2, GROUPS)), dma((2, GROUPS)),
        dma((N_LON,)), dma((N_LON,)),
    ]

    def call(side):
        return pl.pallas_call(
            functools.partial(layer_kernel, side),
            out_shape=jax.ShapeDtypeStruct((CELLS, D), BF16),
            in_specs=[smem] * 2 + [vmem] * 7 + [hbm] * 3,
            out_specs=vmem,
            scratch_shapes=scratch,
            compiler_params=pltpu.CompilerParams(
                collective_id=side, has_side_effects=True, vmem_limit_bytes=56 * 1024 * 1024
            ),
            cost_estimate=pl.CostEstimate(
                flops=6_000_000_000, bytes_accessed=8_000_000, transcendentals=1_000_000
            ),
            name=("columns_east", "columns_west")[side],
        )

    out = lax.cond(
        shift_lon[0] <= 6, call(0), call(1),
        shift_lat, shift_lon, flat(tokens), flat(queries), flat(keys), flat(values),
        norm_gain.reshape(1, D), w_router.T, routes.reshape(CELLS, 2).T,
        w_gate.reshape(D, ff), w_up.reshape(D, ff), w_down.reshape(D, ff),
    )
    return out.reshape(6, 12, 2, D).transpose(2, 0, 1, 3)


def solution(mesh):
    cells = P("exp", "lat", "lon", None)
    weights = P("lon", None, "exp")
    in_specs = (
        cells, cells, cells, cells, P(), P(), P(), P(),
        P("exp", "lat", "lon", None, None), weights, weights, weights,
    )
    return jax.shard_map(
        shards, mesh=mesh, in_specs=in_specs, out_specs=cells, check_vma=False
    )
```

```python
import functools

import jax
import jax.numpy as jnp
from jax import lax
from jax.experimental import pallas as pl
from jax.experimental.pallas import tpu as pltpu
from jax.sharding import PartitionSpec as P

MESH = pl.DeviceIdType.MESH
F32 = jnp.float32
BF16 = jnp.bfloat16

CELLS = 144
D = 1024
LANES = 128
RUNS = CELLS * D // LANES
FB = 256
NF = D // FB
HEAD_DIM = 32
HEADS_FB = FB // HEAD_DIM
N_LON, N_LAT, N_EXP = 32, 4, 4
EXPERTS = 32
CAP = 12
GROUPS = 8
GROUP_ROWS = 4 * CAP
STACK = 4 * GROUP_ROWS
HALF = 72
SENT = 224
BACK = 80
DOWN = ((96, 48), (64, 80), (16, 128))
UP = ((0, 128), (0, 80), (0, 48))
STEPS = (0, 1, 7, 4, 2, 6, 3, 5)


def iota(shape, dim):
    return lax.broadcasted_iota(jnp.int32, shape, dim)


def div12(n):
    return (n * 43691) >> 19


def div24(n):
    return (n * 43691) >> 20


def hot(mask, dtype=BF16):
    return jnp.where(mask, 1.0, 0.0).astype(dtype)


def dot(a, b):
    return jnp.dot(a, b, preferred_element_type=F32)


def dot_nt(a, b):
    return lax.dot_general(a, b, (((1,), (1,)), ((), ())), preferred_element_type=F32)


def remote(src, dst, send, recv, **where):
    return pltpu.make_async_remote_copy(
        src_ref=src, dst_ref=dst, send_sem=send, recv_sem=recv,
        device_id=where, device_id_type=MESH,
    )


def stacked(swap, rows):
    blocks = jnp.concatenate([rows[:, f * FB : (f + 1) * FB] for f in range(NF)], axis=0)
    return dot(swap[...], blocks).astype(BF16).reshape(4, GROUP_ROWS, FB)


def set_swap(swap):
    n, at = iota((STACK, STACK), 0), iota((STACK, STACK), 1)
    outer = div24(n) >> 1
    rest = n - 48 * outer
    inner = div12(rest)
    swap[...] = hot(48 * inner + 12 * outer + (rest - 12 * inner) == at)


def layer_kernel(
    side, mode, slat, slon, tok, qry, key, val, gain, wr, routes, wg_hbm, wu_hbm, wd_hbm, out,
    mid, sbuf, pick0, pick1, comb, wd_t,
    wd, qkv, sent, got, w3, from_up, from_dn, qx, full, lret, lret_got, ret, ret_got, nrm,
    m_low, m_high, m_row, m_in, bias, bias_own, pick_lon, put_lon, pick_ret, put_ret,
    untile, swap, disp, hot0, hot1, rows_out,
    wg, wu, mbuf, rbuf, sback, yback, bbuf, z, pr, rlb, rab, ybuf,
    w_sem, lat_s, lat_r, lon_s, lon_r, ret_s, ret_r, lret_s, lret_r,
    mem_s, mem_r, y_s, y_r, by_s, by_r, bm_s, bm_r,
    ag_s, ag_r, fw_s, fw_r, rl_s, rl_r, ra_s, ra_r,
):
    me = lax.axis_index("lon")
    lat = lax.axis_index("lat")
    east, west = lax.rem(me + 1, N_LON), lax.rem(me + N_LON - 1, N_LON)
    below, above = lax.rem(lat + 1, N_LAT), lax.rem(lat + N_LAT - 1, N_LAT)
    first = 0 if side else 12
    owned = (NF - 1, 0, NF - 1)[mode]
    moved = pl.ds(*(DOWN[0], None, UP[2])[mode]) if owned else None

    ex = lax.axis_index("exp")
    right, left = lax.rem(ex + 1, N_EXP), lax.rem(ex + N_EXP - 1, N_EXP)

    barrier = pltpu.get_barrier_semaphore()

    def signal(axis, to):
        pl.semaphore_signal(barrier, inc=1, device_id={axis: to}, device_id_type=MESH)

    @pl.loop(1, N_LON)
    def _(o):
        signal("lon", lax.rem(me + o, N_LON))

    for axis, to in (("lat", below), ("lat", above), ("exp", right), ("exp", left)):
        signal(axis, to)

    weights = [
        pltpu.make_async_copy(h, v, w_sem.at[n])
        for n, (h, v) in enumerate(((wg_hbm, wg), (wu_hbm, wu), (wd_hbm, wd)))
    ]
    for copy in weights:
        copy.start()

    def lon_copy(f):
        return remote(sent.at[f], got.at[f], lon_s.at[f], lon_r.at[f], lon=(east, west)[side])

    def ret_copy(f):
        return remote(ret.at[f], ret_got.at[f], ret_s.at[f], ret_r.at[f], lon=(west, east)[side])

    def lat_copy(way, f):
        rows = pl.ds(*(DOWN, UP)[way][mode])
        dst, to = ((from_up, below), (from_dn, above))[way]
        return remote(
            w3.at[f, 1:3, rows], dst.at[f, 1:3, rows], lat_s.at[way, f], lat_r.at[way, f], lat=to
        )

    def own_copy(f):
        way = mode // 2
        dst, to = ((from_up, below), (from_dn, above))[way]
        return remote(
            w3.at[f, :, moved], dst.at[f, :, moved], lat_s.at[way, f], lat_r.at[way, f], lat=to
        )

    def lret_copy(f):
        return remote(
            lret.at[f], lret_got.at[f], lret_s.at[f], lret_r.at[f],
            lat=(above, None, below)[mode],
        )

    n, at = iota((LANES, LANES), 0), iota((LANES, LANES), 1)
    untile[...] = hot(((n & 15) >> 1) * 16 + (n >> 4) * 2 + (n & 1) == at)

    def dense(ref, store):
        for b in range(CELLS // 16):
            rows = dot(untile[...], ref[b * LANES : (b + 1) * LANES])
            for j in range(D // LANES):
                f, c = j // 2, (j % 2) * LANES
                store(f, slice(b * 16, b * 16 + 16), slice(c, c + LANES), rows[j * 16 : j * 16 + 16])

    s, t = slat[0], slon[0]
    for a, ref in enumerate((qry, key, val)):

        def to_qkv(f, rows, cols, part, a=a):
            qkv[f, a * CELLS + rows.start : a * CELLS + rows.stop, cols] = part.astype(BF16)

        dense(ref, to_qkv)
    n, at = iota((SENT, 3 * CELLS), 0), iota((SENT, 3 * CELLS), 1)
    a = jnp.where(n >= HALF, 1, 0) + jnp.where(n >= 2 * HALF, 1, 0)
    m = n - HALF * a
    row = div12(m)
    source = a * CELLS + row * 24 + first + (m - 12 * row)
    pick_lon[...] = hot((source == at) & (n < 3 * HALF))
    for f in range(NF):
        sent[f] = dot(pick_lon[...], qkv[f]).astype(BF16)

    pl.semaphore_wait(barrier, N_LON - 1 + 4)
    for f in range(NF):
        lon_copy(f).start()

    n = iota((CELLS, FB), 0)
    row = div24(n)
    rest = n - 24 * row
    at_top, at_bottom = jnp.where(lat == 0, 100, 0), jnp.where(lat == N_LAT - 1, 100, 0)
    m_row[...] = hot(row < 6 - s, F32)
    m_low[...] = hot(row < 6 - s + at_top, F32)
    m_high[...] = hot(row < 6 - s - at_bottom, F32)
    columns = (rest >> 1) < 12 - t
    m_in[...] = hot(columns, F32) if side == 0 else 1.0 - hot(columns, F32)

    shape = (3 * CELLS, 3 * CELLS + SENT)
    n, at = iota(shape, 0), iota(shape, 1)
    a = jnp.where(n >= CELLS, 1, 0) + jnp.where(n >= 2 * CELLS, 1, 0)
    m = n - CELLS * a
    row = div24(m)
    rest = m - 24 * row
    inside = (rest >> 1) < 12 - t if side == 0 else (rest >> 1) >= 12 - t
    put_lon[...] = hot(
        at == jnp.where(inside, n, 3 * CELLS + HALF * a + row * 12 + rest - first)
    )
    head_of = iota((CELLS, FB), 1) >> 5

    for f in range(NF):
        lon_copy(f).wait_recv()
        cells = dot(put_lon[...], jnp.concatenate([qkv[f], got[f]], axis=0))
        w3[f] = cells.astype(BF16).reshape(3, CELLS, FB)
        if f < owned:
            own_copy(f).start()
        else:

            @pl.when(lat < N_LAT - 1)
            def _(f=f):
                lat_copy(0, f).start()

            @pl.when(lat > 0)
            def _(f=f):
                lat_copy(1, f).start()

    def to_mid(f, rows, cols, part):
        mid[f, rows, cols] = part

    dense(tok, to_mid)

    krow = div24(iota((CELLS, CELLS), 1))
    upper = m_row[:, :CELLS] > 0.5
    low = jnp.where(krow < 6 - s + 100 * lat, 0.0, -1e30)
    high = jnp.where(krow >= 6 - s - 100 * (N_LAT - 1 - lat), 0.0, -1e30)
    bias[...] = jnp.where(upper, low, high)
    if owned:
        both = 100 * lat if mode == 0 else 100 * (N_LAT - 1 - lat)
        bias_own[...] = jnp.where(
            upper,
            jnp.where(krow < 6 - s + both, 0.0, -1e30),
            jnp.where(krow >= 6 - s - both, 0.0, -1e30),
        )

    n, at = iota((BACK, CELLS), 0), iota((BACK, CELLS), 1)
    row = div12(n)
    pick_ret[...] = hot(row * 24 + first + (n - 12 * row) == at)
    n, at = iota((CELLS, BACK), 0), iota((CELLS, BACK), 1)
    row = div24(n)
    rest = n - 24 * row - first
    put_ret[...] = hot((row * 12 + rest == at) & (rest >= 0) & (rest < 12))

    tri = hot(iota((CELLS, CELLS), 0) > iota((CELLS, CELLS), 1))
    n, at = iota((CELLS, CELLS), 0), iota((CELLS, CELLS), 1)
    eye = n == at
    ordered = (n & 1) * HALF + (n >> 1) == at
    e = iota((CELLS, EXPERTS), 1)
    order = (((e & 15) >> 1) * 4 + (e >> 4) * 2 + (e & 1)).astype(F32)
    e = e.astype(F32)
    before = jnp.zeros((1, EXPERTS), F32)
    spread = jnp.zeros((EXPERTS * CAP, CELLS), F32)
    for k, (one, pick) in enumerate(((hot0, pick0), (hot1, pick1))):
        named = jnp.broadcast_to(routes[k : k + 1, :].astype(F32), (CELLS, CELLS))
        chosen = jnp.sum(jnp.where(ordered, named, 0.0), axis=1, keepdims=True)
        oh = hot(jnp.broadcast_to(chosen, (CELLS, EXPERTS)) == e, F32)
        one[...] = oh
        slot = jnp.sum((dot(tri, oh.astype(BF16)) + before) * oh, axis=1, keepdims=True)
        before = before + jnp.sum(oh, axis=0, keepdims=True)
        pos = slot + CAP * jnp.sum(oh * order, axis=1, keepdims=True)
        pick[...] = hot(
            jnp.broadcast_to(pos, (CELLS, EXPERTS * CAP))
            == iota((CELLS, EXPERTS * CAP), 1).astype(F32)
        )
        pos_row = jnp.sum(
            jnp.where(eye, jnp.broadcast_to(pos, (CELLS, CELLS)), 0.0), axis=0, keepdims=True
        )
        spread = spread + hot(
            jnp.broadcast_to(pos_row, (EXPERTS * CAP, CELLS))
            == iota((EXPERTS * CAP, CELLS), 0).astype(F32),
            F32,
        )
    disp[...] = spread.astype(BF16)
    set_swap(swap)

    for copy in weights:
        copy.wait()
    wd_t[...] = wd[...].T

    def spread_heads(q):
        q = q.astype(F32)
        for h in range(HEADS_FB):
            qx[h * CELLS : (h + 1) * CELLS] = jnp.where(head_of == h, q, 0.0).astype(BF16)

    def attend(windows, bias_ref):
        s_w = [dot_nt(qx[...], w[0]) for w in windows]
        probs, scale = [], []
        for h in range(HEADS_FB):
            part = [x[h * CELLS : (h + 1) * CELLS] for x in s_w]
            score = part[0]
            if len(part) == 2:
                score = jnp.where(m_row[:, :CELLS] > 0.5, part[0], part[1])
            score = score * HEAD_DIM ** (-0.5) + bias_ref[...]
            weight = jnp.exp(score - jnp.max(score, axis=1, keepdims=True))
            scale.append(1.0 / jnp.sum(weight, axis=1, keepdims=True))
            probs.append(weight.astype(BF16))
        probs = jnp.concatenate(probs, axis=0)
        o_w = [dot(probs, w[1]) for w in windows]
        total = jnp.zeros((CELLS, FB), F32)
        for h in range(HEADS_FB):
            part = [x[h * CELLS : (h + 1) * CELLS] for x in o_w]
            heads = part[0]
            if len(part) == 2:
                heads = jnp.where(m_row[...] > 0.5, part[0], part[1])
            total = jnp.where(head_of == h, heads * scale[h], total)
        return total

    def send_home(f, total):
        ret[f] = dot(pick_ret[...], total.astype(BF16)).astype(BF16)
        ret_copy(f).start()
        mid[f] = mid[f] + jnp.where(m_in[...] > 0.5, total, 0.0)

    def attend_exchanged(f):
        @pl.when(lat > 0)
        def _():
            lat_copy(0, f).wait_recv()

        @pl.when(lat < N_LAT - 1)
        def _():
            lat_copy(1, f).wait_recv()

        spread_heads(w3[f, 0])
        low, high = [], []
        for a in (1, 2):
            own, up, dn = (r[f, a].astype(F32) for r in (w3, from_up, from_dn))
            low.append(jnp.where(m_low[...] > 0.5, own, up).astype(BF16))
            high.append(jnp.where(m_high[...] > 0.5, dn, own).astype(BF16))
        send_home(f, attend((low, high), bias))

    def attend_owned(f):
        own_copy(f).wait_recv()
        win = []
        for a in range(3):
            own = w3[f, a].astype(F32)
            if mode == 0:
                win.append(jnp.where(m_row[...] > 0.5, own, from_up[f, a].astype(F32)))
            else:
                win.append(jnp.where(m_row[...] > 0.5, from_dn[f, a].astype(F32), own))
        spread_heads(win[0])
        total = attend(((win[1].astype(BF16), win[2].astype(BF16)),), bias_own)
        full[f] = total
        lret[f] = total[moved.start : moved.start + moved.size].astype(BF16)
        lret_copy(f).start()

    def finish_owned(f):
        lret_copy(f).wait_recv()
        total = full[f]
        back = lret_got[f].astype(F32)
        a, b = moved.start, moved.start + moved.size
        mine = m_row[a:b] > 0.5
        if mode == 0:
            total = jnp.concatenate([total[:a], jnp.where(mine, total[a:b], back)], axis=0)
        else:
            total = jnp.concatenate([jnp.where(mine, back, total[a:b]), total[b:]], axis=0)
        send_home(f, total)

    if owned:

        @pl.loop(0, owned)
        def _(f):
            attend_owned(f)

            @pl.when(f > 0)
            def _():
                finish_owned(f - 1)

        attend_exchanged(owned)
        finish_owned(owned - 1)
    else:

        @pl.loop(0, NF)
        def _(f):
            attend_exchanged(f)

    for f in range(NF):
        ret_copy(f).wait_recv()
        back_home = dot(put_ret[...], ret_got[f])
        mid[f] = mid[f] + jnp.where(m_in[...] > 0.5, 0.0, back_home)

    square = sum(jnp.sum(mid[f] * mid[f], axis=1, keepdims=True) for f in range(NF))
    inv = lax.rsqrt(square * (1.0 / D) + 1e-06)
    for f in range(NF):
        cols = slice(f * FB, (f + 1) * FB)
        nrm[:, cols] = (mid[f] * inv * gain[:, cols]).astype(BF16)
    logits = dot_nt(nrm[...], wr[...])
    gates = [
        jax.nn.sigmoid(jnp.sum(logits * one[...], axis=1, keepdims=True)) for one in (hot0, hot1)
    ]
    for k in range(2):
        comb[k] = jnp.broadcast_to(gates[k] / (gates[0] + gates[1]), (CELLS, 128))

    rows_out[...] = dot(disp[...], nrm[...]).astype(BF16)
    for g in range(GROUPS):
        sbuf[g * 4 : g * 4 + 4] = stacked(
            swap, rows_out[g * GROUP_ROWS : (g + 1) * GROUP_ROWS]
        )

    zl, y, c = me // 16, lax.rem(me // 2, 8), lax.rem(me, 2)
    mm = zl * 2 + c
    members = [lax.rem(mm + o, 4) for o in range(1, 4)]

    def lon_of(m, at_y):
        return (m // 2) * 16 + at_y * 2 + lax.rem(m, 2)

    def four(q):
        return pl.ds(4 * q, 4)

    def there(i):
        return lax.rem(y + STEPS[i], GROUPS)

    def group(i):
        return lax.rem(y + GROUPS - STEPS[i], GROUPS)

    def mem_copy(to_y, m):
        return remote(
            sbuf.at[4 * to_y + m], mbuf.at[4 * to_y + mm],
            mem_s.at[4 * to_y + m], mem_r.at[4 * to_y + mm], lon=lon_of(m, y),
        )

    def mem_from(to_y, m):
        return remote(
            sbuf.at[4 * to_y + m], mbuf.at[4 * to_y + m],
            mem_s.at[4 * to_y + m], mem_r.at[4 * to_y + m], lon=lon_of(m, y),
        )

    def y_copy(to_y):
        return remote(
            mbuf.at[four(to_y)], rbuf.at[four(y)], y_s.at[to_y], y_r.at[y], lon=lon_of(mm, to_y)
        )

    def y_from(at_y):
        return remote(
            mbuf.at[four(at_y)], rbuf.at[four(at_y)], y_s.at[at_y], y_r.at[at_y],
            lon=lon_of(mm, at_y),
        )

    def back_y(to_y):
        return remote(
            sback.at[four(to_y)], yback.at[four(y)], by_s.at[to_y], by_r.at[y],
            lon=lon_of(mm, to_y),
        )

    def back_y_from(at_y):
        return remote(
            sback.at[four(at_y)], yback.at[four(at_y)], by_s.at[at_y], by_r.at[at_y],
            lon=lon_of(mm, at_y),
        )

    def back_mem(at_y, m):
        return remote(
            yback.at[4 * at_y + m], bbuf.at[4 * at_y + mm],
            bm_s.at[4 * at_y + m], bm_r.at[4 * at_y + mm], lon=lon_of(m, y),
        )

    def back_mem_from(at_y, m):
        return remote(
            yback.at[4 * at_y + m], bbuf.at[4 * at_y + m],
            bm_s.at[4 * at_y + m], bm_r.at[4 * at_y + m], lon=lon_of(m, y),
        )

    def unstacked(blocks):
        rows = dot(swap[...], blocks.reshape(STACK, FB)).astype(BF16)
        return [rows[f * GROUP_ROWS : (f + 1) * GROUP_ROWS] for f in range(NF)]

    for i in range(GROUPS):
        for m in members:
            mem_copy(there(i), m).start()
    for i in range(GROUPS):
        q = 4 * there(i) + mm
        mbuf[q] = sbuf[q]

    def ag(way, i):
        return remote(
            z.at[0, i], z.at[1 + way, i], ag_s.at[way, i], ag_r.at[way, i],
            exp=(right, left)[way],
        )

    def fw(i):
        way = i % 2
        return remote(
            z.at[1 + way, i], z.at[3, i], fw_s.at[i], fw_r.at[i], exp=(right, left)[way]
        )

    def forward(i):
        ag(0, i).wait_recv()
        ag(1, i).wait_recv()
        fw(i).start()

    def ffn(plane, half):
        rows = z[plane, 4 * half : 4 * half + 4].reshape(STACK, D)
        gate = dot(rows, wg[...])
        up = dot(rows, wu[...])
        hidden = (gate / (1.0 + jnp.exp(-gate)) * up).astype(BF16)
        down = dot(hidden, wd_t[...]).astype(BF16)
        pr[plane, 4 * half : 4 * half + 4] = down.reshape(4, GROUP_ROWS, D)

    def rl(i):
        return remote(
            pr.at[3, i], rlb.at[i], rl_s.at[i], rl_r.at[i], exp=(right, left)[i % 2]
        )

    def ra(way, i):
        return remote(
            pr.at[2 - way, i], rab.at[way, i], ra_s.at[way, i], ra_r.at[way, i],
            exp=(right, left)[way],
        )

    def halves(half):
        return range(4 * half, 4 * half + 4)

    def direct(half):
        for i in halves(half):
            ra(1 - i % 2, i).start()

    def relay(half):
        for i in halves(half):
            fw(i).wait_recv()
        ffn(3, half)
        for i in halves(half):
            rl(i).start()

    def relayed(half):
        for i in halves(half):
            way = i % 2
            rl(i).wait_recv()
            pr[2 - way, i] = (pr[2 - way, i].astype(F32) + rlb[i].astype(F32)).astype(BF16)
            ra(way, i).start()

    def finish(half):
        for i in halves(half):
            ra(0, i).wait_recv()
            ra(1, i).wait_recv()
            rows = pr[0, i].astype(F32) + rab[0, i].astype(F32) + rab[1, i].astype(F32)
            blocks = stacked(swap, rows.astype(BF16))
            g = group(i)
            if i == 0:
                yback[four(y)] = blocks
            else:
                sback[four(g)] = blocks
                back_y(g).start()

    def to_members(half):
        for i in halves(half):
            at_y = there(i)
            if i > 0:
                back_y_from(at_y).wait_recv()
            for m in members:
                back_mem(at_y, m).start()
            bbuf[4 * at_y + mm] = yback[4 * at_y + mm]

    def gathered(i):
        for f, rows in enumerate(unstacked(rbuf[four(group(i))])):
            z[0, i, :, f * FB : (f + 1) * FB] = rows
        ag(0, i).start()
        ag(1, i).start()

    for i in range(GROUPS):
        for m in members:
            mem_from(there(i), m).wait_recv()
        if i == 0:
            rbuf[four(y)] = mbuf[four(y)]
            gathered(0)
        else:
            y_copy(there(i)).start()
    for i in range(1, GROUPS):
        y_from(group(i)).wait_recv()
        gathered(i)
        if i >= 2:
            forward(i - 2)
        if i >= 5:
            ffn(i - 5, 0)
    direct(0)
    forward(6)
    relay(0)
    forward(7)
    relay(1)
    ffn(1, 1)
    ffn(2, 1)
    direct(1)
    relayed(0)
    ffn(0, 1)
    finish(0)
    relayed(1)
    to_members(0)
    finish(1)
    to_members(1)

    for i in range(GROUPS):
        at_y = there(i)
        for m in members:
            back_mem_from(at_y, m).wait_recv()
        at = pl.ds(pl.multiple_of(at_y * GROUP_ROWS, 16), GROUP_ROWS)
        for f, rows in enumerate(unstacked(bbuf[four(at_y)])):
            ybuf[at, f * FB : (f + 1) * FB] = rows
    for f in range(NF):
        cols = slice(f * FB, (f + 1) * FB)
        moe = comb[0, :, :1] * dot(pick0[...], ybuf[:, cols])
        moe = moe + comb[1, :, :1] * dot(pick1[...], ybuf[:, cols])
        out[:, cols] = (mid[f] + moe).astype(BF16)
    for f in range(NF):
        lon_copy(f).wait_send()
        ret_copy(f).wait_send()
    for f in range(owned):
        own_copy(f).wait_send()
        lret_copy(f).wait_send()

    @pl.when(lat < N_LAT - 1)
    def _():
        for f in range(owned, NF):
            lat_copy(0, f).wait_send()

    @pl.when(lat > 0)
    def _():
        for f in range(owned, NF):
            lat_copy(1, f).wait_send()

    for i in range(GROUPS):
        fw(i).wait_send()
        rl(i).wait_send()
        for way in range(2):
            ag(way, i).wait_send()
            ra(way, i).wait_send()

    for i in range(GROUPS):
        at_y = there(i)
        if i > 0:
            y_copy(at_y).wait_send()
            back_y(group(i)).wait_send()
        for m in members:
            mem_copy(at_y, m).wait_send()
            back_mem(at_y, m).wait_send()


def shards(
    tokens, queries, keys, values, shift_lat, shift_lon, norm_gain, w_router, routes,
    w_gate, w_up, w_down,
):
    def flat(x):
        return x.reshape(2, 6, 12, D // LANES, LANES).transpose(1, 2, 3, 0, 4).reshape(RUNS, LANES)

    smem = pl.BlockSpec(memory_space=pltpu.SMEM)
    vmem = pl.BlockSpec(memory_space=pltpu.VMEM)
    hbm = pl.BlockSpec(memory_space=pl.ANY)
    dma = pltpu.SemaphoreType.DMA
    slots = EXPERTS * CAP
    ff = w_gate.shape[2]

    def buf(*shape):
        return pltpu.VMEM(shape, BF16)

    def buf32(*shape):
        return pltpu.VMEM(shape, F32)

    def params(number):
        return pltpu.CompilerParams(
            collective_id=number, has_side_effects=True, vmem_limit_bytes=56 * 1024 * 1024
        )

    kv = buf(NF, 3, CELLS, FB)
    mask = buf32(CELLS, FB)
    square = buf32(CELLS, CELLS)

    lon = buf(N_LON, GROUP_ROWS, FB)
    planes = buf(N_EXP, GROUPS, GROUP_ROWS, D)
    weight = buf(D, ff)
    pairs, one, each = dma((2, GROUPS)), dma((GROUPS,)), dma((N_LON,))
    scratch = [
        buf32(NF, CELLS, FB), lon, buf(CELLS, slots), buf(CELLS, slots), buf32(2, CELLS, 128),
        buf(ff, D), weight, buf(NF, 3 * CELLS, FB), buf(NF, SENT, FB), buf(NF, SENT, FB),
        kv, kv, kv, buf(HEADS_FB * CELLS, FB), buf32(NF, CELLS, FB),
        buf(NF, 48, FB), buf(NF, 48, FB), buf(NF, BACK, FB), buf(NF, BACK, FB), buf(CELLS, D),
        mask, mask, mask, mask, square, square,
        buf(SENT, 3 * CELLS), buf(3 * CELLS, 3 * CELLS + SENT),
        buf(BACK, CELLS), buf(CELLS, BACK),
        buf(LANES, LANES), buf(STACK, STACK), buf(slots, CELLS),
        buf32(CELLS, EXPERTS), buf32(CELLS, EXPERTS), buf(slots, D),
        weight, weight, lon, lon, lon, lon, lon, planes, planes,
        buf(GROUPS, GROUP_ROWS, D), buf(2, GROUPS, GROUP_ROWS, D), buf(slots, D),
        dma((3,)), dma((2, NF)), dma((2, NF)),
        dma((NF,)), dma((NF,)), dma((NF,)), dma((NF,)), dma((NF,)), dma((NF,)),
        each, each, one, one, one, one, each, each,
        pairs, pairs, one, one, one, one, pairs, pairs,
    ]

    def layer(side, mode):
        return pl.pallas_call(
            functools.partial(layer_kernel, side, mode),
            out_shape=jax.ShapeDtypeStruct((CELLS, D), BF16),
            in_specs=[smem] * 2 + [vmem] * 7 + [hbm] * 3,
            out_specs=vmem,
            scratch_shapes=scratch,
            compiler_params=params(side * 3 + mode),
            cost_estimate=pl.CostEstimate(
                flops=6_000_000_000, bytes_accessed=8_000_000, transcendentals=2_000_000
            ),
            name=f"layer_{side}_{mode}",
        )

    turn = 3 * (shift_lon[0] > 6).astype(jnp.int32)
    turn = turn + (shift_lat[0] > 2).astype(jnp.int32) + (shift_lat[0] > 3).astype(jnp.int32)
    out = lax.switch(
        turn, [layer(side, mode) for side in range(2) for mode in range(3)],
        shift_lat, shift_lon, flat(tokens), flat(queries), flat(keys), flat(values),
        norm_gain.reshape(1, D), w_router.T, routes.reshape(CELLS, 2).T,
        w_gate.reshape(D, ff), w_up.reshape(D, ff), w_down.reshape(D, ff),
    )
    return out.reshape(6, 12, 2, D).transpose(2, 0, 1, 3)


def solution(mesh):
    cells = P("exp", "lat", "lon", None)
    weights = P("lon", None, "exp")
    in_specs = (
        cells, cells, cells, cells, P(), P(), P(), P(),
        P("exp", "lat", "lon", None, None), weights, weights, weights,
    )
    return jax.shard_map(
        shards, mesh=mesh, in_specs=in_specs, out_specs=cells, check_vma=False
    )
```

```python
import functools

import jax
import jax.numpy as jnp
from jax import lax
from jax.experimental import pallas as pl
from jax.experimental.pallas import tpu as pltpu
from jax.sharding import PartitionSpec as P

MESH = pl.DeviceIdType.MESH
F32 = jnp.float32
BF16 = jnp.bfloat16

CELLS = 144
D = 1024
LANES = 128
RUNS = CELLS * D // LANES
FB = 256
NF = D // FB
HEAD_DIM = 32
HEADS_FB = FB // HEAD_DIM
N_LON, N_LAT, N_EXP = 32, 4, 4
EXPERTS = 32
CAP = 12
GROUPS = 8
GROUP_ROWS = 4 * CAP
STACK = 4 * GROUP_ROWS
HALF = 72
SENT = 224
BACK = 80
ORDER = ((0, 0), (1, 0), (0, 1), (0, 3), (1, 1), (1, 3), (0, 2), (1, 2))


def iota(shape, dim):
    return lax.broadcasted_iota(jnp.int32, shape, dim)


def div12(n):
    return (n * 43691) >> 19


def div24(n):
    return (n * 43691) >> 20


def hot(mask, dtype=BF16):
    return jnp.where(mask, 1.0, 0.0).astype(dtype)


def dot(a, b):
    return jnp.dot(a, b, preferred_element_type=F32)


def dot_nt(a, b):
    return lax.dot_general(a, b, (((1,), (1,)), ((), ())), preferred_element_type=F32)


def layer_kernel(
    side, slat, slon, tok, qry, key, val, gain, wr, routes, wg_hbm, wu_hbm, wd_hbm, out,
    wg, wu, wd, wd_t, qkv, sent, got, kv, kv_up, kv_dn, qx, ret, ret_got, mid, nrm,
    m_low, m_high, m_row, m_in, bias, pick_lon, put_lon, pick_ret, put_ret, untile, swap,
    pick0, pick1, disp, hot0, hot1, sbuf, rbuf, z, pr, rlb, rab, bbuf, ybuf, comb,
    w_sem, lat_s, lat_r, lon_s, lon_r, ret_s, ret_r, a2a_s, a2a_r, ag_s, ag_r, fw_s, fw_r,
    rl_s, rl_r, ra_s, ra_r, bk_s, bk_r,
):
    me = lax.axis_index("lon")
    lat = lax.axis_index("lat")
    ex = lax.axis_index("exp")
    right, left = lax.rem(ex + 1, N_EXP), lax.rem(ex + N_EXP - 1, N_EXP)
    east, west = lax.rem(me + 1, N_LON), lax.rem(me + N_LON - 1, N_LON)
    first = 0 if side else 12

    barrier = pltpu.get_barrier_semaphore()

    @pl.loop(1, N_LON)
    def _(o):
        pl.semaphore_signal(
            barrier, inc=1, device_id={"lon": lax.rem(me + o, N_LON)}, device_id_type=MESH
        )

    for axis, at, count in (("lat", lat, N_LAT), ("exp", ex, N_EXP)):
        for o in (1, count - 1):
            pl.semaphore_signal(
                barrier, inc=1, device_id={axis: lax.rem(at + o, count)}, device_id_type=MESH
            )

    weights = [
        pltpu.make_async_copy(h, v, w_sem.at[n])
        for n, (h, v) in enumerate(((wg_hbm, wg), (wu_hbm, wu), (wd_hbm, wd)))
    ]
    for copy in weights:
        copy.start()

    def remote(src, dst, send, recv, **where):
        return pltpu.make_async_remote_copy(
            src_ref=src, dst_ref=dst, send_sem=send, recv_sem=recv,
            device_id=where, device_id_type=MESH,
        )

    def lon_copy(f):
        return remote(sent.at[f], got.at[f], lon_s.at[f], lon_r.at[f], lon=(east, west)[side])

    def ret_copy(f):
        return remote(ret.at[f], ret_got.at[f], ret_s.at[f], ret_r.at[f], lon=(west, east)[side])

    def lat_copy(way, f):
        rows, dst, to = (
            (pl.ds(16, 128), kv_up, lax.rem(lat + 1, N_LAT)),
            (pl.ds(0, 128), kv_dn, lax.rem(lat + N_LAT - 1, N_LAT)),
        )[way]
        return remote(
            kv.at[f, :, rows], dst.at[f, :, rows], lat_s.at[way, f], lat_r.at[way, f], lat=to
        )

    n, at = iota((LANES, LANES), 0), iota((LANES, LANES), 1)
    untile[...] = hot(((n & 15) >> 1) * 16 + (n >> 4) * 2 + (n & 1) == at)

    def dense(ref, store):
        for b in range(CELLS // 16):
            rows = dot(untile[...], ref[b * LANES : (b + 1) * LANES])
            for j in range(D // LANES):
                f, c = j // 2, (j % 2) * LANES
                store(f, slice(b * 16, b * 16 + 16), slice(c, c + LANES), rows[j * 16 : j * 16 + 16])

    s, t = slat[0], slon[0]
    for a, ref in enumerate((qry, key, val)):

        def to_qkv(f, rows, cols, part, a=a):
            qkv[f, a * CELLS + rows.start : a * CELLS + rows.stop, cols] = part.astype(BF16)

        dense(ref, to_qkv)
    n, at = iota((SENT, 3 * CELLS), 0), iota((SENT, 3 * CELLS), 1)
    a = jnp.where(n >= HALF, 1, 0) + jnp.where(n >= 2 * HALF, 1, 0)
    m = n - HALF * a
    row = div12(m)
    source = a * CELLS + row * 24 + first + (m - 12 * row)
    pick_lon[...] = hot((source == at) & (n < 3 * HALF))
    for f in range(NF):
        sent[f] = dot(pick_lon[...], qkv[f]).astype(BF16)

    pl.semaphore_wait(barrier, N_LON - 1 + 4)
    for f in range(NF):
        lon_copy(f).start()

    n = iota((CELLS, FB), 0)
    row = div24(n)
    rest = n - 24 * row
    at_top, at_bottom = jnp.where(lat == 0, 100, 0), jnp.where(lat == N_LAT - 1, 100, 0)
    m_row[...] = hot(row < 6 - s, F32)
    m_low[...] = hot(row < 6 - s + at_top, F32)
    m_high[...] = hot(row < 6 - s - at_bottom, F32)
    columns = (rest >> 1) < 12 - t
    m_in[...] = hot(columns, F32) if side == 0 else 1.0 - hot(columns, F32)

    shape = (3 * CELLS, 3 * CELLS + SENT)
    n, at = iota(shape, 0), iota(shape, 1)
    a = jnp.where(n >= CELLS, 1, 0) + jnp.where(n >= 2 * CELLS, 1, 0)
    m = n - CELLS * a
    row = div24(m)
    rest = m - 24 * row
    inside = (rest >> 1) < 12 - t if side == 0 else (rest >> 1) >= 12 - t
    put_lon[...] = hot(
        at == jnp.where(inside, n, 3 * CELLS + HALF * a + row * 12 + rest - first)
    )
    head_of = iota((CELLS, FB), 1) >> 5

    def own_columns(f):
        lon_copy(f).wait_recv()
        cells = dot(put_lon[...], jnp.concatenate([qkv[f], got[f]], axis=0))
        kv[f, 0] = cells[CELLS : 2 * CELLS].astype(BF16)
        kv[f, 1] = cells[2 * CELLS :].astype(BF16)

        @pl.when(lat < N_LAT - 1)
        def _():
            lat_copy(0, f).start()

        @pl.when(lat > 0)
        def _():
            lat_copy(1, f).start()

        for h in range(HEADS_FB):
            qx[f, h * CELLS : (h + 1) * CELLS] = jnp.where(
                head_of == h, cells[:CELLS], 0.0
            ).astype(BF16)

    @pl.loop(0, NF)
    def _(f):
        own_columns(f)

    def to_mid(f, rows, cols, part):
        mid[f, rows, cols] = part

    dense(tok, to_mid)

    krow = div24(iota((CELLS, CELLS), 1))
    low = jnp.where(krow < 6 - s + 100 * lat, 0.0, -1e30)
    high = jnp.where(krow >= 6 - s - 100 * (N_LAT - 1 - lat), 0.0, -1e30)
    bias[...] = jnp.where(m_row[:, :CELLS] > 0.5, low, high)

    n, at = iota((BACK, CELLS), 0), iota((BACK, CELLS), 1)
    row = div12(n)
    pick_ret[...] = hot(row * 24 + first + (n - 12 * row) == at)
    n, at = iota((CELLS, BACK), 0), iota((CELLS, BACK), 1)
    row = div24(n)
    rest = n - 24 * row - first
    put_ret[...] = hot((row * 12 + rest == at) & (rest >= 0) & (rest < 12))

    tri = hot(iota((CELLS, CELLS), 0) > iota((CELLS, CELLS), 1))
    n, at = iota((CELLS, CELLS), 0), iota((CELLS, CELLS), 1)
    eye = n == at
    ordered = (n & 1) * HALF + (n >> 1) == at
    e = iota((CELLS, EXPERTS), 1).astype(F32)
    before = jnp.zeros((1, EXPERTS), F32)
    spread = jnp.zeros((EXPERTS * CAP, CELLS), F32)
    for k, (one, pick) in enumerate(((hot0, pick0), (hot1, pick1))):
        named = jnp.broadcast_to(routes[k : k + 1, :].astype(F32), (CELLS, CELLS))
        chosen = jnp.sum(jnp.where(ordered, named, 0.0), axis=1, keepdims=True)
        oh = hot(jnp.broadcast_to(chosen, (CELLS, EXPERTS)) == e, F32)
        one[...] = oh
        slot = jnp.sum((dot(tri, oh.astype(BF16)) + before) * oh, axis=1, keepdims=True)
        before = before + jnp.sum(oh, axis=0, keepdims=True)
        pos = slot + CAP * chosen
        pick[...] = hot(
            jnp.broadcast_to(pos, (CELLS, EXPERTS * CAP))
            == iota((CELLS, EXPERTS * CAP), 1).astype(F32)
        )
        pos_row = jnp.sum(
            jnp.where(eye, jnp.broadcast_to(pos, (CELLS, CELLS)), 0.0), axis=0, keepdims=True
        )
        spread = spread + hot(
            jnp.broadcast_to(pos_row, (EXPERTS * CAP, CELLS))
            == iota((EXPERTS * CAP, CELLS), 0).astype(F32),
            F32,
        )
    disp[...] = spread.astype(BF16)
    n, at = iota((STACK, STACK), 0), iota((STACK, STACK), 1)
    outer = div24(n) >> 1
    rest = n - 48 * outer
    inner = div12(rest)
    swap[...] = hot(48 * inner + 12 * outer + (rest - 12 * inner) == at)

    for copy in weights:
        copy.wait()
    wd_t[...] = wd[...].T

    def attend(f):
        @pl.when(lat > 0)
        def _():
            lat_copy(0, f).wait_recv()

        @pl.when(lat < N_LAT - 1)
        def _():
            lat_copy(1, f).wait_recv()

        win = []
        for a in range(2):
            own, up, dn = (r[f, a].astype(F32) for r in (kv, kv_up, kv_dn))
            win.append(
                (
                    jnp.where(m_low[...] > 0.5, own, up).astype(BF16),
                    jnp.where(m_high[...] > 0.5, dn, own).astype(BF16),
                )
            )
        spread_q = qx[f]
        s_w = [dot_nt(spread_q, w) for w in win[0]]
        first_row = m_row[:, :CELLS] > 0.5
        probs, scale = [], []
        for h in range(HEADS_FB):
            part = [x[h * CELLS : (h + 1) * CELLS] for x in s_w]
            score = jnp.where(first_row, part[0], part[1]) * HEAD_DIM ** (-0.5) + bias[...]
            weight = jnp.exp(score - jnp.max(score, axis=1, keepdims=True))
            scale.append(1.0 / jnp.sum(weight, axis=1, keepdims=True))
            probs.append(weight.astype(BF16))
        probs = jnp.concatenate(probs, axis=0)
        o_w = [dot(probs, w) for w in win[1]]
        first_row = m_row[...] > 0.5
        total = jnp.zeros((CELLS, FB), F32)
        for h in range(HEADS_FB):
            part = [x[h * CELLS : (h + 1) * CELLS] for x in o_w]
            heads = jnp.where(first_row, part[0], part[1]) * scale[h]
            total = jnp.where(head_of == h, heads, total)
        ret[f] = dot(pick_ret[...], total.astype(BF16)).astype(BF16)
        ret_copy(f).start()
        mid[f] = mid[f] + jnp.where(m_in[...] > 0.5, total, 0.0)

    @pl.loop(0, NF)
    def _(f):
        attend(f)

    for f in range(NF):
        ret_copy(f).wait_recv()
        back_home = dot(put_ret[...], ret_got[f])
        mid[f] = mid[f] + jnp.where(m_in[...] > 0.5, 0.0, back_home)

    square = sum(jnp.sum(mid[f] * mid[f], axis=1, keepdims=True) for f in range(NF))
    inv = lax.rsqrt(square * (1.0 / D) + 1e-06)
    for f in range(NF):
        cols = slice(f * FB, (f + 1) * FB)
        nrm[:, cols] = (mid[f] * inv * gain[:, cols]).astype(BF16)
    logits = dot_nt(nrm[...], wr[...])
    gates = [
        jax.nn.sigmoid(jnp.sum(logits * one[...], axis=1, keepdims=True)) for one in (hot0, hot1)
    ]
    for k in range(2):
        comb[k] = jnp.broadcast_to(gates[k] / (gates[0] + gates[1]), (CELLS, 128))

    zl, yp, sm = me // 16, lax.rem(me // 4, 4), lax.rem(me, 4)

    def group(i):
        dz, dy = ORDER[i]
        return lax.rem(zl + dz, 2) * 4 + lax.rem(yp + dy, 4)

    def a2a(d):
        return remote(sbuf.at[d], rbuf.at[me], a2a_s.at[d], a2a_r.at[me], lon=d)

    def a2a_from(d):
        return remote(sbuf.at[d], rbuf.at[d], a2a_s.at[d], a2a_r.at[d], lon=d)

    def back(d):
        return remote(sbuf.at[d], bbuf.at[me], bk_s.at[d], bk_r.at[me], lon=d)

    def back_from(d):
        return remote(sbuf.at[d], bbuf.at[d], bk_s.at[d], bk_r.at[d], lon=d)

    def stacked(rows):
        blocks = jnp.concatenate([rows[:, f * FB : (f + 1) * FB] for f in range(NF)], axis=0)
        return dot(swap[...], blocks).astype(BF16).reshape(4, GROUP_ROWS, FB)

    def unstacked(blocks):
        rows = dot(swap[...], blocks.reshape(STACK, FB)).astype(BF16)
        return [rows[f * GROUP_ROWS : (f + 1) * GROUP_ROWS] for f in range(NF)]

    ybuf[...] = dot(disp[...], nrm[...]).astype(BF16)
    for i in range(GROUPS):
        g = group(i)
        sbuf[pl.ds(g * 4, 4)] = stacked(
            ybuf[pl.ds(pl.multiple_of(g * GROUP_ROWS, 16), GROUP_ROWS)]
        )
    rbuf[me] = sbuf[me]
    for i in range(GROUPS):
        g = group(i)
        for o in range(4):
            if not (i == 0 and o == 0):
                a2a(g * 4 + lax.rem(sm + o, 4)).start()

    def ag(way, i):
        return remote(
            z.at[0, i], z.at[1 + way, i], ag_s.at[way, i], ag_r.at[way, i],
            exp=(right, left)[way],
        )

    def fw(i):
        way = i % 2
        return remote(
            z.at[1 + way, i], z.at[3, i], fw_s.at[i], fw_r.at[i], exp=(right, left)[way]
        )

    def forward(i):
        ag(0, i).wait_recv()
        ag(1, i).wait_recv()
        fw(i).start()

    def ffn(plane, count, half):
        planes, part = pl.ds(plane, count), pl.ds(4 * half, 4)
        rows = z[planes, part].reshape(count * STACK, D)
        gate = dot(rows, wg[...])
        up = dot(rows, wu[...])
        hidden = (gate / (1.0 + jnp.exp(-gate)) * up).astype(BF16)
        down = dot(hidden, wd_t[...]).astype(BF16)
        pr[planes, part] = down.reshape(count, 4, GROUP_ROWS, D)

    def rl(i):
        return remote(
            pr.at[3, i], rlb.at[i], rl_s.at[i], rl_r.at[i], exp=(right, left)[i % 2]
        )

    def ra(way, i):
        return remote(
            pr.at[2 - way, i], rab.at[way, i], ra_s.at[way, i], ra_r.at[way, i],
            exp=(right, left)[way],
        )

    def halves(half):
        return range(4 * half, 4 * half + 4)

    def direct(i):
        ra(1 - i % 2, i).start()

    def relay(half):
        for i in halves(half):
            fw(i).wait_recv()
        ffn(3, 1, half)
        for i in halves(half):
            rl(i).start()

    def relayed(i):
        way = i % 2
        rl(i).wait_recv()
        pr[2 - way, i] = (pr[2 - way, i].astype(F32) + rlb[i].astype(F32)).astype(BF16)
        ra(way, i).start()

    def finish(half):
        for i in halves(half):
            ra(0, i).wait_recv()
            ra(1, i).wait_recv()
            rows = pr[0, i].astype(F32) + rab[0, i].astype(F32) + rab[1, i].astype(F32)
            blocks = stacked(rows.astype(BF16))
            g = group(i)
            if i == 0:
                for o in range(1, 4):
                    a2a(g * 4 + lax.rem(sm + o, 4)).wait_send()
            else:
                for o in range(4):
                    a2a(g * 4 + lax.rem(sm + o, 4)).wait_send()
            sbuf[pl.ds(g * 4, 4)] = blocks
            for o in range(4):
                d = g * 4 + lax.rem(sm + o, 4)
                if i == 0 and o == 0:
                    bbuf[d] = sbuf[d]
                else:
                    back(d).start()

    for i in range(GROUPS):
        g = group(i)
        for o in range(4):
            if not (i == 0 and o == 0):
                a2a_from(g * 4 + lax.rem(sm + o, 4)).wait_recv()
        for f, rows in enumerate(unstacked(rbuf[pl.ds(g * 4, 4)])):
            z[0, i, :, f * FB : (f + 1) * FB] = rows
        ag(0, i).start()
        ag(1, i).start()
        if i >= 2:
            forward(i - 2)
        if i == 5:
            ffn(0, 1, 0)
        if i == 6:
            ffn(1, 2, 0)
            for k in halves(0):
                direct(k)
    forward(6)
    relay(0)
    forward(7)
    for i in halves(0):
        relayed(i)
    relay(1)
    ffn(1, 2, 1)
    for i in halves(1):
        direct(i)
        relayed(i)
    finish(0)
    ffn(0, 1, 1)
    finish(1)

    for i in range(GROUPS):
        g = group(i)
        for o in range(4):
            if not (i == 0 and o == 0):
                back_from(g * 4 + lax.rem(sm + o, 4)).wait_recv()
        at = pl.ds(pl.multiple_of(g * GROUP_ROWS, 16), GROUP_ROWS)
        for f, rows in enumerate(unstacked(bbuf[pl.ds(g * 4, 4)])):
            ybuf[at, f * FB : (f + 1) * FB] = rows
    for f in range(NF):
        cols = slice(f * FB, (f + 1) * FB)
        moe = comb[0, :, :1] * dot(pick0[...], ybuf[:, cols])
        moe = moe + comb[1, :, :1] * dot(pick1[...], ybuf[:, cols])
        out[:, cols] = (mid[f] + moe).astype(BF16)
    for f in range(NF):
        lon_copy(f).wait_send()
        ret_copy(f).wait_send()

    @pl.when(lat < N_LAT - 1)
    def _():
        for f in range(NF):
            lat_copy(0, f).wait_send()

    @pl.when(lat > 0)
    def _():
        for f in range(NF):
            lat_copy(1, f).wait_send()

    for i in range(GROUPS):
        fw(i).wait_send()
        rl(i).wait_send()
        for way in range(2):
            ag(way, i).wait_send()
            ra(way, i).wait_send()

    @pl.loop(1, N_LON)
    def _(o):
        back(lax.rem(me + o, N_LON)).wait_send()


def shards(
    tokens, queries, keys, values, shift_lat, shift_lon, norm_gain, w_router, routes,
    w_gate, w_up, w_down,
):
    def flat(x):
        return x.reshape(2, 6, 12, D // LANES, LANES).transpose(1, 2, 3, 0, 4).reshape(RUNS, LANES)

    smem = pl.BlockSpec(memory_space=pltpu.SMEM)
    vmem = pl.BlockSpec(memory_space=pltpu.VMEM)
    hbm = pl.BlockSpec(memory_space=pl.ANY)
    dma = pltpu.SemaphoreType.DMA
    kv = pltpu.VMEM((NF, 2, CELLS, FB), BF16)
    lon = pltpu.VMEM((NF, SENT, FB), BF16)
    ret = pltpu.VMEM((NF, BACK, FB), BF16)
    blocks = pltpu.VMEM((N_LON, GROUP_ROWS, FB), BF16)
    planes = pltpu.VMEM((N_EXP, GROUPS, GROUP_ROWS, D), BF16)
    mask = pltpu.VMEM((CELLS, FB), F32)
    slots = EXPERTS * CAP
    ff = w_gate.shape[2]
    scratch = [
        pltpu.VMEM((D, ff), BF16), pltpu.VMEM((D, ff), BF16), pltpu.VMEM((D, ff), BF16),
        pltpu.VMEM((ff, D), BF16),
        pltpu.VMEM((NF, 3 * CELLS, FB), BF16),
        lon, lon, kv, kv, kv,
        pltpu.VMEM((NF, HEADS_FB * CELLS, FB), BF16),
        ret, ret,
        pltpu.VMEM((NF, CELLS, FB), F32),
        pltpu.VMEM((CELLS, D), BF16),
        mask, mask, mask, mask,
        pltpu.VMEM((CELLS, CELLS), F32),
        pltpu.VMEM((SENT, 3 * CELLS), BF16), pltpu.VMEM((3 * CELLS, 3 * CELLS + SENT), BF16),
        pltpu.VMEM((BACK, CELLS), BF16), pltpu.VMEM((CELLS, BACK), BF16),
        pltpu.VMEM((LANES, LANES), BF16),
        pltpu.VMEM((STACK, STACK), BF16),
        pltpu.VMEM((CELLS, slots), BF16), pltpu.VMEM((CELLS, slots), BF16),
        pltpu.VMEM((slots, CELLS), BF16),
        pltpu.VMEM((CELLS, EXPERTS), F32), pltpu.VMEM((CELLS, EXPERTS), F32),
        blocks, blocks, planes, planes,
        pltpu.VMEM((GROUPS, GROUP_ROWS, D), BF16),
        pltpu.VMEM((2, GROUPS, GROUP_ROWS, D), BF16),
        blocks,
        pltpu.VMEM((slots, D), BF16),
        pltpu.VMEM((2, CELLS, 128), F32),
        dma((3,)),
        dma((2, NF)), dma((2, NF)), dma((NF,)), dma((NF,)), dma((NF,)), dma((NF,)),
        dma((N_LON,)), dma((N_LON,)),
        dma((2, GROUPS)), dma((2, GROUPS)), dma((GROUPS,)), dma((GROUPS,)),
        dma((GROUPS,)), dma((GROUPS,)), dma((2, GROUPS)), dma((2, GROUPS)),
        dma((N_LON,)), dma((N_LON,)),
    ]

    def call(side):
        return pl.pallas_call(
            functools.partial(layer_kernel, side),
            out_shape=jax.ShapeDtypeStruct((CELLS, D), BF16),
            in_specs=[smem] * 2 + [vmem] * 7 + [hbm] * 3,
            out_specs=vmem,
            scratch_shapes=scratch,
            compiler_params=pltpu.CompilerParams(
                collective_id=side, has_side_effects=True, vmem_limit_bytes=56 * 1024 * 1024
            ),
            cost_estimate=pl.CostEstimate(
                flops=6_000_000_000, bytes_accessed=8_000_000, transcendentals=1_000_000
            ),
            name=("columns_east", "columns_west")[side],
        )

    out = lax.cond(
        shift_lon[0] <= 6, call(0), call(1),
        shift_lat, shift_lon, flat(tokens), flat(queries), flat(keys), flat(values),
        norm_gain.reshape(1, D), w_router.T, routes.reshape(CELLS, 2).T,
        w_gate.reshape(D, ff), w_up.reshape(D, ff), w_down.reshape(D, ff),
    )
    return out.reshape(6, 12, 2, D).transpose(2, 0, 1, 3)


def solution(mesh):
    cells = P("exp", "lat", "lon", None)
    weights = P("lon", None, "exp")
    in_specs = (
        cells, cells, cells, cells, P(), P(), P(), P(),
        P("exp", "lat", "lon", None, None), weights, weights, weights,
    )
    return jax.shard_map(
        shards, mesh=mesh, in_specs=in_specs, out_specs=cells, check_vma=False
    )
```

```python
import functools

import jax
import jax.numpy as jnp
from jax import lax
from jax.experimental import pallas as pl
from jax.experimental.pallas import tpu as pltpu
from jax.sharding import PartitionSpec as P

MESH = pl.DeviceIdType.MESH
F32 = jnp.float32
BF16 = jnp.bfloat16

CELLS = 144
D = 1024
LANES = 128
RUNS = CELLS * D // LANES
FB = 256
NF = D // FB
HEAD_DIM = 32
HEADS_FB = FB // HEAD_DIM
N_LON, N_LAT, N_EXP = 32, 4, 4
EXPERTS = 32
CAP = 12
GROUPS = 8
GROUP_ROWS = 4 * CAP
STACK = 4 * GROUP_ROWS
HALF = 72
SENT = 224
BACK = 80
ORDER = ((0, 0), (1, 0), (0, 1), (0, 3), (1, 1), (1, 3), (0, 2), (1, 2))


def iota(shape, dim):
    return lax.broadcasted_iota(jnp.int32, shape, dim)


def div12(n):
    return (n * 43691) >> 19


def div24(n):
    return (n * 43691) >> 20


def hot(mask, dtype=BF16):
    return jnp.where(mask, 1.0, 0.0).astype(dtype)


def dot(a, b):
    return jnp.dot(a, b, preferred_element_type=F32)


def dot_nt(a, b):
    return lax.dot_general(a, b, (((1,), (1,)), ((), ())), preferred_element_type=F32)


def layer_kernel(
    side, slat, slon, tok, qry, key, val, gain, wr, routes, wg_hbm, wu_hbm, wd_hbm, out,
    wg, wu, wd, wd_t, qkv, sent, got, kv, kv_up, kv_dn, qx, ret, ret_got, mid, nrm,
    m_low, m_high, m_row, m_in, bias, pick_lon, put_lon, pick_ret, put_ret, untile, swap,
    pick0, pick1, disp, hot0, hot1, sbuf, rbuf, z, pr, rlb, rab, bbuf, ybuf, comb,
    w_sem, lat_s, lat_r, lon_s, lon_r, ret_s, ret_r, a2a_s, a2a_r, ag_s, ag_r, fw_s, fw_r,
    rl_s, rl_r, ra_s, ra_r, bk_s, bk_r,
):
    me = lax.axis_index("lon")
    lat = lax.axis_index("lat")
    ex = lax.axis_index("exp")
    right, left = lax.rem(ex + 1, N_EXP), lax.rem(ex + N_EXP - 1, N_EXP)
    east, west = lax.rem(me + 1, N_LON), lax.rem(me + N_LON - 1, N_LON)
    first = 0 if side else 12

    barrier = pltpu.get_barrier_semaphore()

    @pl.loop(1, N_LON)
    def _(o):
        pl.semaphore_signal(
            barrier, inc=1, device_id={"lon": lax.rem(me + o, N_LON)}, device_id_type=MESH
        )

    for axis, at, count in (("lat", lat, N_LAT), ("exp", ex, N_EXP)):
        for o in (1, count - 1):
            pl.semaphore_signal(
                barrier, inc=1, device_id={axis: lax.rem(at + o, count)}, device_id_type=MESH
            )

    weights = [
        pltpu.make_async_copy(h, v, w_sem.at[n])
        for n, (h, v) in enumerate(((wg_hbm, wg), (wu_hbm, wu), (wd_hbm, wd)))
    ]
    for copy in weights:
        copy.start()

    def remote(src, dst, send, recv, **where):
        return pltpu.make_async_remote_copy(
            src_ref=src, dst_ref=dst, send_sem=send, recv_sem=recv,
            device_id=where, device_id_type=MESH,
        )

    def lon_copy(f):
        return remote(sent.at[f], got.at[f], lon_s.at[f], lon_r.at[f], lon=(east, west)[side])

    def ret_copy(f):
        return remote(ret.at[f], ret_got.at[f], ret_s.at[f], ret_r.at[f], lon=(west, east)[side])

    def lat_copy(way, f):
        rows, dst, to = (
            (pl.ds(16, 128), kv_up, lax.rem(lat + 1, N_LAT)),
            (pl.ds(0, 128), kv_dn, lax.rem(lat + N_LAT - 1, N_LAT)),
        )[way]
        return remote(
            kv.at[f, :, rows], dst.at[f, :, rows], lat_s.at[way, f], lat_r.at[way, f], lat=to
        )

    n, at = iota((LANES, LANES), 0), iota((LANES, LANES), 1)
    untile[...] = hot(((n & 15) >> 1) * 16 + (n >> 4) * 2 + (n & 1) == at)

    def dense(ref, store):
        for b in range(CELLS // 16):
            rows = dot(untile[...], ref[b * LANES : (b + 1) * LANES])
            for j in range(D // LANES):
                f, c = j // 2, (j % 2) * LANES
                store(f, slice(b * 16, b * 16 + 16), slice(c, c + LANES), rows[j * 16 : j * 16 + 16])

    s, t = slat[0], slon[0]
    for a, ref in enumerate((qry, key, val)):

        def to_qkv(f, rows, cols, part, a=a):
            qkv[f, a * CELLS + rows.start : a * CELLS + rows.stop, cols] = part.astype(BF16)

        dense(ref, to_qkv)
    n, at = iota((SENT, 3 * CELLS), 0), iota((SENT, 3 * CELLS), 1)
    a = jnp.where(n >= HALF, 1, 0) + jnp.where(n >= 2 * HALF, 1, 0)
    m = n - HALF * a
    row = div12(m)
    source = a * CELLS + row * 24 + first + (m - 12 * row)
    pick_lon[...] = hot((source == at) & (n < 3 * HALF))
    for f in range(NF):
        sent[f] = dot(pick_lon[...], qkv[f]).astype(BF16)

    pl.semaphore_wait(barrier, N_LON - 1 + 4)
    for f in range(NF):
        lon_copy(f).start()

    n = iota((CELLS, FB), 0)
    row = div24(n)
    rest = n - 24 * row
    at_top, at_bottom = jnp.where(lat == 0, 100, 0), jnp.where(lat == N_LAT - 1, 100, 0)
    m_row[...] = hot(row < 6 - s, F32)
    m_low[...] = hot(row < 6 - s + at_top, F32)
    m_high[...] = hot(row < 6 - s - at_bottom, F32)
    columns = (rest >> 1) < 12 - t
    m_in[...] = hot(columns, F32) if side == 0 else 1.0 - hot(columns, F32)

    shape = (3 * CELLS, 3 * CELLS + SENT)
    n, at = iota(shape, 0), iota(shape, 1)
    a = jnp.where(n >= CELLS, 1, 0) + jnp.where(n >= 2 * CELLS, 1, 0)
    m = n - CELLS * a
    row = div24(m)
    rest = m - 24 * row
    inside = (rest >> 1) < 12 - t if side == 0 else (rest >> 1) >= 12 - t
    put_lon[...] = hot(
        at == jnp.where(inside, n, 3 * CELLS + HALF * a + row * 12 + rest - first)
    )
    head_of = iota((CELLS, FB), 1) >> 5

    def own_columns(f):
        lon_copy(f).wait_recv()
        cells = dot(put_lon[...], jnp.concatenate([qkv[f], got[f]], axis=0))
        kv[f, 0] = cells[CELLS : 2 * CELLS].astype(BF16)
        kv[f, 1] = cells[2 * CELLS :].astype(BF16)

        @pl.when(lat < N_LAT - 1)
        def _():
            lat_copy(0, f).start()

        @pl.when(lat > 0)
        def _():
            lat_copy(1, f).start()

        for h in range(HEADS_FB):
            qx[f, h * CELLS : (h + 1) * CELLS] = jnp.where(
                head_of == h, cells[:CELLS], 0.0
            ).astype(BF16)

    @pl.loop(0, NF)
    def _(f):
        own_columns(f)

    def to_mid(f, rows, cols, part):
        mid[f, rows, cols] = part

    dense(tok, to_mid)

    krow = div24(iota((CELLS, CELLS), 1))
    low = jnp.where(krow < 6 - s + 100 * lat, 0.0, -1e30)
    high = jnp.where(krow >= 6 - s - 100 * (N_LAT - 1 - lat), 0.0, -1e30)
    bias[...] = jnp.where(m_row[:, :CELLS] > 0.5, low, high)

    n, at = iota((BACK, CELLS), 0), iota((BACK, CELLS), 1)
    row = div12(n)
    pick_ret[...] = hot(row * 24 + first + (n - 12 * row) == at)
    n, at = iota((CELLS, BACK), 0), iota((CELLS, BACK), 1)
    row = div24(n)
    rest = n - 24 * row - first
    put_ret[...] = hot((row * 12 + rest == at) & (rest >= 0) & (rest < 12))

    tri = hot(iota((CELLS, CELLS), 0) > iota((CELLS, CELLS), 1))
    n, at = iota((CELLS, CELLS), 0), iota((CELLS, CELLS), 1)
    eye = n == at
    ordered = (n & 1) * HALF + (n >> 1) == at
    e = iota((CELLS, EXPERTS), 1).astype(F32)
    before = jnp.zeros((1, EXPERTS), F32)
    spread = jnp.zeros((EXPERTS * CAP, CELLS), F32)
    for k, (one, pick) in enumerate(((hot0, pick0), (hot1, pick1))):
        named = jnp.broadcast_to(routes[k : k + 1, :].astype(F32), (CELLS, CELLS))
        chosen = jnp.sum(jnp.where(ordered, named, 0.0), axis=1, keepdims=True)
        oh = hot(jnp.broadcast_to(chosen, (CELLS, EXPERTS)) == e, F32)
        one[...] = oh
        slot = jnp.sum((dot(tri, oh.astype(BF16)) + before) * oh, axis=1, keepdims=True)
        before = before + jnp.sum(oh, axis=0, keepdims=True)
        pos = slot + CAP * chosen
        pick[...] = hot(
            jnp.broadcast_to(pos, (CELLS, EXPERTS * CAP))
            == iota((CELLS, EXPERTS * CAP), 1).astype(F32)
        )
        pos_row = jnp.sum(
            jnp.where(eye, jnp.broadcast_to(pos, (CELLS, CELLS)), 0.0), axis=0, keepdims=True
        )
        spread = spread + hot(
            jnp.broadcast_to(pos_row, (EXPERTS * CAP, CELLS))
            == iota((EXPERTS * CAP, CELLS), 0).astype(F32),
            F32,
        )
    disp[...] = spread.astype(BF16)
    n, at = iota((STACK, STACK), 0), iota((STACK, STACK), 1)
    outer = div24(n) >> 1
    rest = n - 48 * outer
    inner = div12(rest)
    swap[...] = hot(48 * inner + 12 * outer + (rest - 12 * inner) == at)

    for copy in weights:
        copy.wait()
    wd_t[...] = wd[...].T

    def attend(f):
        @pl.when(lat > 0)
        def _():
            lat_copy(0, f).wait_recv()

        @pl.when(lat < N_LAT - 1)
        def _():
            lat_copy(1, f).wait_recv()

        win = []
        for a in range(2):
            own, up, dn = (r[f, a].astype(F32) for r in (kv, kv_up, kv_dn))
            win.append(
                (
                    jnp.where(m_low[...] > 0.5, own, up).astype(BF16),
                    jnp.where(m_high[...] > 0.5, dn, own).astype(BF16),
                )
            )
        spread_q = qx[f]
        s_w = [dot_nt(spread_q, w) for w in win[0]]
        first_row = m_row[:, :CELLS] > 0.5
        probs, scale = [], []
        for h in range(HEADS_FB):
            part = [x[h * CELLS : (h + 1) * CELLS] for x in s_w]
            score = jnp.where(first_row, part[0], part[1]) * HEAD_DIM ** (-0.5) + bias[...]
            weight = jnp.exp(score - jnp.max(score, axis=1, keepdims=True))
            scale.append(1.0 / jnp.sum(weight, axis=1, keepdims=True))
            probs.append(weight.astype(BF16))
        probs = jnp.concatenate(probs, axis=0)
        o_w = [dot(probs, w) for w in win[1]]
        first_row = m_row[...] > 0.5
        total = jnp.zeros((CELLS, FB), F32)
        for h in range(HEADS_FB):
            part = [x[h * CELLS : (h + 1) * CELLS] for x in o_w]
            heads = jnp.where(first_row, part[0], part[1]) * scale[h]
            total = jnp.where(head_of == h, heads, total)
        ret[f] = dot(pick_ret[...], total.astype(BF16)).astype(BF16)
        ret_copy(f).start()
        mid[f] = mid[f] + jnp.where(m_in[...] > 0.5, total, 0.0)

    @pl.loop(0, NF)
    def _(f):
        attend(f)

    for f in range(NF):
        ret_copy(f).wait_recv()
        back_home = dot(put_ret[...], ret_got[f])
        mid[f] = mid[f] + jnp.where(m_in[...] > 0.5, 0.0, back_home)

    square = sum(jnp.sum(mid[f] * mid[f], axis=1, keepdims=True) for f in range(NF))
    inv = lax.rsqrt(square * (1.0 / D) + 1e-06)
    for f in range(NF):
        cols = slice(f * FB, (f + 1) * FB)
        nrm[:, cols] = (mid[f] * inv * gain[:, cols]).astype(BF16)
    logits = dot_nt(nrm[...], wr[...])
    gates = [
        jax.nn.sigmoid(jnp.sum(logits * one[...], axis=1, keepdims=True)) for one in (hot0, hot1)
    ]
    for k in range(2):
        comb[k] = jnp.broadcast_to(gates[k] / (gates[0] + gates[1]), (CELLS, 128))

    zl, yp, sm = me // 16, lax.rem(me // 4, 4), lax.rem(me, 4)

    def group(i):
        dz, dy = ORDER[i]
        return lax.rem(zl + dz, 2) * 4 + lax.rem(yp + dy, 4)

    def a2a(d):
        return remote(sbuf.at[d], rbuf.at[me], a2a_s.at[d], a2a_r.at[me], lon=d)

    def a2a_from(d):
        return remote(sbuf.at[d], rbuf.at[d], a2a_s.at[d], a2a_r.at[d], lon=d)

    def back(d):
        return remote(sbuf.at[d], bbuf.at[me], bk_s.at[d], bk_r.at[me], lon=d)

    def back_from(d):
        return remote(sbuf.at[d], bbuf.at[d], bk_s.at[d], bk_r.at[d], lon=d)

    def stacked(rows):
        blocks = jnp.concatenate([rows[:, f * FB : (f + 1) * FB] for f in range(NF)], axis=0)
        return dot(swap[...], blocks).astype(BF16).reshape(4, GROUP_ROWS, FB)

    def unstacked(blocks):
        rows = dot(swap[...], blocks.reshape(STACK, FB)).astype(BF16)
        return [rows[f * GROUP_ROWS : (f + 1) * GROUP_ROWS] for f in range(NF)]

    ybuf[...] = dot(disp[...], nrm[...]).astype(BF16)
    for i in range(GROUPS):
        g = group(i)
        sbuf[pl.ds(g * 4, 4)] = stacked(
            ybuf[pl.ds(pl.multiple_of(g * GROUP_ROWS, 16), GROUP_ROWS)]
        )
        for o in range(4):
            if i == 0 and o == 0:
                rbuf[me] = sbuf[me]
            else:
                a2a(g * 4 + lax.rem(sm + o, 4)).start()

    def ag(way, i):
        return remote(
            z.at[0, i], z.at[1 + way, i], ag_s.at[way, i], ag_r.at[way, i],
            exp=(right, left)[way],
        )

    def fw(i):
        way = i % 2
        return remote(
            z.at[1 + way, i], z.at[3, i], fw_s.at[i], fw_r.at[i], exp=(right, left)[way]
        )

    def forward(i):
        ag(i % 2, i).wait_recv()
        fw(i).start()

    def ffn(plane, count, half):
        planes, part = pl.ds(plane, count), pl.ds(4 * half, 4)
        rows = z[planes, part].reshape(count * STACK, D)
        gate = dot(rows, wg[...])
        up = dot(rows, wu[...])
        hidden = (gate / (1.0 + jnp.exp(-gate)) * up).astype(BF16)
        down = dot(hidden, wd_t[...]).astype(BF16)
        pr[planes, part] = down.reshape(count, 4, GROUP_ROWS, D)

    def rl(i):
        return remote(
            pr.at[3, i], rlb.at[i], rl_s.at[i], rl_r.at[i], exp=(right, left)[i % 2]
        )

    def ra(way, i):
        return remote(
            pr.at[2 - way, i], rab.at[way, i], ra_s.at[way, i], ra_r.at[way, i],
            exp=(right, left)[way],
        )

    def halves(half):
        return range(4 * half, 4 * half + 4)

    def others(half):
        for i in halves(half):
            ag(1 - i % 2, i).wait_recv()

    def direct(i):
        ra(1 - i % 2, i).start()

    def relay(half):
        for i in halves(half):
            fw(i).wait_recv()
        ffn(3, 1, half)
        for i in halves(half):
            rl(i).start()

    def relayed(i):
        way = i % 2
        rl(i).wait_recv()
        pr[2 - way, i] = (pr[2 - way, i].astype(F32) + rlb[i].astype(F32)).astype(BF16)
        ra(way, i).start()

    def finish(half):
        for i in halves(half):
            ra(0, i).wait_recv()
            ra(1, i).wait_recv()
            rows = pr[0, i].astype(F32) + rab[0, i].astype(F32) + rab[1, i].astype(F32)
            blocks = stacked(rows.astype(BF16))
            g = group(i)
            if i == 0:
                for o in range(1, 4):
                    a2a(g * 4 + lax.rem(sm + o, 4)).wait_send()
            else:
                for o in range(4):
                    a2a(g * 4 + lax.rem(sm + o, 4)).wait_send()
            sbuf[pl.ds(g * 4, 4)] = blocks
            for o in range(4):
                d = g * 4 + lax.rem(sm + o, 4)
                if i == 0 and o == 0:
                    bbuf[d] = sbuf[d]
                else:
                    back(d).start()

    for i in range(GROUPS):
        g = group(i)
        for o in range(4):
            if not (i == 0 and o == 0):
                a2a_from(g * 4 + lax.rem(sm + o, 4)).wait_recv()
        for f, rows in enumerate(unstacked(rbuf[pl.ds(g * 4, 4)])):
            z[0, i, :, f * FB : (f + 1) * FB] = rows
        ag(0, i).start()
        ag(1, i).start()
        if i >= 2:
            forward(i - 2)
        if i == 5:
            ffn(0, 1, 0)
        if i == 6:
            others(0)
            ffn(1, 2, 0)
            for k in halves(0):
                direct(k)
    forward(6)
    relay(0)
    forward(7)
    for i in halves(0):
        relayed(i)
    relay(1)
    others(1)
    ffn(1, 2, 1)
    for i in halves(1):
        direct(i)
        relayed(i)
    finish(0)
    ffn(0, 1, 1)
    finish(1)

    for i in range(GROUPS):
        g = group(i)
        for o in range(4):
            if not (i == 0 and o == 0):
                back_from(g * 4 + lax.rem(sm + o, 4)).wait_recv()
        at = pl.ds(pl.multiple_of(g * GROUP_ROWS, 16), GROUP_ROWS)
        for f, rows in enumerate(unstacked(bbuf[pl.ds(g * 4, 4)])):
            ybuf[at, f * FB : (f + 1) * FB] = rows
    for f in range(NF):
        cols = slice(f * FB, (f + 1) * FB)
        moe = comb[0, :, :1] * dot(pick0[...], ybuf[:, cols])
        moe = moe + comb[1, :, :1] * dot(pick1[...], ybuf[:, cols])
        out[:, cols] = (mid[f] + moe).astype(BF16)
    for f in range(NF):
        lon_copy(f).wait_send()
        ret_copy(f).wait_send()

    @pl.when(lat < N_LAT - 1)
    def _():
        for f in range(NF):
            lat_copy(0, f).wait_send()

    @pl.when(lat > 0)
    def _():
        for f in range(NF):
            lat_copy(1, f).wait_send()

    for i in range(GROUPS):
        fw(i).wait_send()
        rl(i).wait_send()
        for way in range(2):
            ag(way, i).wait_send()
            ra(way, i).wait_send()

    @pl.loop(1, N_LON)
    def _(o):
        back(lax.rem(me + o, N_LON)).wait_send()


def shards(
    tokens, queries, keys, values, shift_lat, shift_lon, norm_gain, w_router, routes,
    w_gate, w_up, w_down,
):
    def flat(x):
        return x.reshape(2, 6, 12, D // LANES, LANES).transpose(1, 2, 3, 0, 4).reshape(RUNS, LANES)

    smem = pl.BlockSpec(memory_space=pltpu.SMEM)
    vmem = pl.BlockSpec(memory_space=pltpu.VMEM)
    hbm = pl.BlockSpec(memory_space=pl.ANY)
    dma = pltpu.SemaphoreType.DMA
    kv = pltpu.VMEM((NF, 2, CELLS, FB), BF16)
    lon = pltpu.VMEM((NF, SENT, FB), BF16)
    ret = pltpu.VMEM((NF, BACK, FB), BF16)
    blocks = pltpu.VMEM((N_LON, GROUP_ROWS, FB), BF16)
    planes = pltpu.VMEM((N_EXP, GROUPS, GROUP_ROWS, D), BF16)
    mask = pltpu.VMEM((CELLS, FB), F32)
    slots = EXPERTS * CAP
    ff = w_gate.shape[2]
    scratch = [
        pltpu.VMEM((D, ff), BF16), pltpu.VMEM((D, ff), BF16), pltpu.VMEM((D, ff), BF16),
        pltpu.VMEM((ff, D), BF16),
        pltpu.VMEM((NF, 3 * CELLS, FB), BF16),
        lon, lon, kv, kv, kv,
        pltpu.VMEM((NF, HEADS_FB * CELLS, FB), BF16),
        ret, ret,
        pltpu.VMEM((NF, CELLS, FB), F32),
        pltpu.VMEM((CELLS, D), BF16),
        mask, mask, mask, mask,
        pltpu.VMEM((CELLS, CELLS), F32),
        pltpu.VMEM((SENT, 3 * CELLS), BF16), pltpu.VMEM((3 * CELLS, 3 * CELLS + SENT), BF16),
        pltpu.VMEM((BACK, CELLS), BF16), pltpu.VMEM((CELLS, BACK), BF16),
        pltpu.VMEM((LANES, LANES), BF16),
        pltpu.VMEM((STACK, STACK), BF16),
        pltpu.VMEM((CELLS, slots), BF16), pltpu.VMEM((CELLS, slots), BF16),
        pltpu.VMEM((slots, CELLS), BF16),
        pltpu.VMEM((CELLS, EXPERTS), F32), pltpu.VMEM((CELLS, EXPERTS), F32),
        blocks, blocks, planes, planes,
        pltpu.VMEM((GROUPS, GROUP_ROWS, D), BF16),
        pltpu.VMEM((2, GROUPS, GROUP_ROWS, D), BF16),
        blocks,
        pltpu.VMEM((slots, D), BF16),
        pltpu.VMEM((2, CELLS, 128), F32),
        dma((3,)),
        dma((2, NF)), dma((2, NF)), dma((NF,)), dma((NF,)), dma((NF,)), dma((NF,)),
        dma((N_LON,)), dma((N_LON,)),
        dma((2, GROUPS)), dma((2, GROUPS)), dma((GROUPS,)), dma((GROUPS,)),
        dma((GROUPS,)), dma((GROUPS,)), dma((2, GROUPS)), dma((2, GROUPS)),
        dma((N_LON,)), dma((N_LON,)),
    ]

    def call(side):
        return pl.pallas_call(
            functools.partial(layer_kernel, side),
            out_shape=jax.ShapeDtypeStruct((CELLS, D), BF16),
            in_specs=[smem] * 2 + [vmem] * 7 + [hbm] * 3,
            out_specs=vmem,
            scratch_shapes=scratch,
            compiler_params=pltpu.CompilerParams(
                collective_id=side, has_side_effects=True, vmem_limit_bytes=56 * 1024 * 1024
            ),
            cost_estimate=pl.CostEstimate(
                flops=6_000_000_000, bytes_accessed=8_000_000, transcendentals=1_000_000
            ),
            name=("columns_east", "columns_west")[side],
        )

    out = lax.cond(
        shift_lon[0] <= 6, call(0), call(1),
        shift_lat, shift_lon, flat(tokens), flat(queries), flat(keys), flat(values),
        norm_gain.reshape(1, D), w_router.T, routes.reshape(CELLS, 2).T,
        w_gate.reshape(D, ff), w_up.reshape(D, ff), w_down.reshape(D, ff),
    )
    return out.reshape(6, 12, 2, D).transpose(2, 0, 1, 3)


def solution(mesh):
    cells = P("exp", "lat", "lon", None)
    weights = P("lon", None, "exp")
    in_specs = (
        cells, cells, cells, cells, P(), P(), P(), P(),
        P("exp", "lat", "lon", None, None), weights, weights, weights,
    )
    return jax.shard_map(
        shards, mesh=mesh, in_specs=in_specs, out_specs=cells, check_vma=False
    )
```
